32 devices in a mesh: box: 8 (over z, x), src: 4 (over y, core).
Axes of the slice: x: 2, y: 2, z: 4, core: 2. Of those that a mesh axis runs over, the one named last changes fastest.
Arguments:
- source_field: bfloat16 [512, 65536], P('src', 'box'), parts along dimension 0, may hold values from -6 to 6
- project_mats: bfloat16 [512, 128], P('box'), may hold values from -0.5 to 0.5
- local_mats: bfloat16 [8, 2, 512, 64], P(None, None, 'box'), may hold values from -0.75 to 0.75
- cross_mats: bfloat16 [6, 2, 512, 64], P(None, None, 'box'), may hold values from -0.75 to 0.75
- angles: bfloat16 [14, 65536], P(None, 'box'), may hold values from -3.140625 to 3.140625
- evaluate_mats: bfloat16 [1024, 64], P('box'), may hold values from -0.75 to 0.75
Outputs:
- image_blocks: bfloat16 [512, 65536], P('src', 'box'), parts along dimension 0
The draws below stay inside these ranges and needn't reach their ends.
There are 4 independent parts, one for each index of `src`. The reference program is written for one: setup_inputs(seed, part) draws one part's arguments, and reference() takes and returns one part's arrays. A program takes and returns all parts, laid end to end along the dimension named above; an argument that names none is the same for every part. Nothing has to cross between parts.
All inputs are finite; a program needn't handle non-finite values.
Results may differ from the reference program's by a relative error of at most 0.024.
Values may be sent and summed in bfloat16 or wider, within the bound.
A program may use at most 128 MiB of HBM per device.

```python
import jax
import jax.numpy as jnp

R = 64
Q = 128
BOX_DEV = 8192
LOCAL = 8
LEVELS = 6
BOXES = 65536
N_BOX = 8


def level_of(key, extent, cuts, smallest, high):
    loudness, own = 1.0, jax.random.fold_in(key, 6)
    for axis_at, parts in cuts:
        heights = jnp.exp(jax.random.uniform(jax.random.fold_in(own, axis_at), (parts,), jnp.float32, smallest / len(cuts), high / len(cuts)))
        loudness = loudness * jnp.repeat(heights, extent[axis_at] // parts).reshape([-1 if axis == axis_at else 1 for axis in range(len(extent))])
    return loudness


def centred(key, shape, width, bound, cuts=(), kind=jnp.bfloat16):
    drawn = width * jax.random.normal(key, shape, jnp.float32)
    if cuts:
        drawn = drawn * level_of(key, shape, cuts, -0.22, 0.18)
    return jnp.clip(drawn, -bound, bound).astype(kind)


def setup_inputs(seed: int = 0, part: int = 0) -> dict:
    keys = jax.random.split(jax.random.key(seed), 7)
    own_keys = jax.random.split(jax.random.fold_in(keys[6], part), 7)
    return {
        "source_field": centred(own_keys[0], (Q, BOXES), 1.0, 6.0, ((1, 8),)),
        "project_mats": centred(keys[1], (N_BOX * R, Q), Q ** -0.5, 0.5, ((0, 8),)),
        "local_mats": centred(keys[2], (LOCAL, 2, N_BOX * R, R), R ** -0.5, 0.75, ((2, 8),)),
        "cross_mats": centred(keys[3], (LEVELS, 2, N_BOX * R, R), R ** -0.5, 0.75, ((2, 8),)),
        "angles": jnp.clip(jax.random.uniform(keys[4], (LOCAL + LEVELS, BOXES), jnp.float32, -3.140625, 3.140625), -3.140625, 3.140625).astype(jnp.bfloat16),
        "evaluate_mats": centred(keys[5], (N_BOX * Q, R), R ** -0.5, 0.75, ((0, 8),)),
    }


def flip_last(values, pair_span):
    full_shape = values.shape
    leading = full_shape[:-1]
    reshaped = values.reshape(leading + (full_shape[-1] // (2 * pair_span), 2, pair_span))
    return jnp.flip(reshaped, axis=-2).reshape(full_shape)


def combine(matrices, current, partner, phase_row):
    blocks = matrices.astype(jnp.float32).reshape(2, N_BOX, R, R)
    own_term = jnp.einsum('dij,jdt->idt', blocks[0], current.astype(jnp.float32))
    partner_term = jnp.einsum('dij,jdt->idt', blocks[1], partner.astype(jnp.float32))
    return (jnp.cos(phase_row)[None] * own_term + jnp.sin(phase_row)[None] * partner_term).astype(jnp.bfloat16)


def reference(source_field, project_mats, local_mats, cross_mats, angles, evaluate_mats):
    field_cube = source_field.astype(jnp.float32).reshape(Q, N_BOX, BOX_DEV)
    projector = project_mats.astype(jnp.float32).reshape(N_BOX, R, Q)
    current = jnp.einsum('diq,qdt->idt', projector, field_cube).astype(jnp.bfloat16)
    phases = angles.astype(jnp.float32).reshape(LOCAL + LEVELS, N_BOX, BOX_DEV)
    local_bits = (BOX_DEV & -BOX_DEV).bit_length() - 1
    box_bits = N_BOX.bit_length() - 1
    for level_idx in range(LOCAL):
        pair_span = 1 << (level_idx % local_bits)
        partner = flip_last(current, pair_span)
        current = combine(local_mats[level_idx], current, partner, phases[level_idx])
    for level_idx in range(LEVELS):
        level_bit = (box_bits - 1 - level_idx) % box_bits
        flat = current.reshape(R, N_BOX * BOX_DEV)
        partner = flip_last(flat, BOX_DEV << level_bit).reshape(R, N_BOX, BOX_DEV)
        current = combine(cross_mats[level_idx], current, partner, phases[LOCAL + level_idx])
    group_size = BOX_DEV // N_BOX
    switched = current.reshape(R, N_BOX, N_BOX, group_size).transpose(0, 2, 1, 3).reshape(R, N_BOX, BOX_DEV)
    evaluator = evaluate_mats.astype(jnp.float32).reshape(N_BOX, Q, R)
    pixels_out = jnp.einsum('gqr,rgs->qgs', evaluator, switched.astype(jnp.float32))
    return pixels_out.reshape(Q, N_BOX * BOX_DEV).astype(jnp.bfloat16)
```

```python
import functools

import jax
import jax.numpy as jnp
from jax import lax
from jax.experimental import pallas as pl
from jax.experimental.pallas import tpu as pltpu
from jax.sharding import PartitionSpec as P

MESH = pl.DeviceIdType.MESH
F32 = jnp.float32
BF16 = jnp.bfloat16
LANES = 128
TILE = 16
UNIT = 256


def swapped(x, axis, distance):
    return lax.ppermute(x, axis, [(i, i ^ 1 << distance) for i in range(lax.axis_size(axis))])


def flip_last(values, pair_span):
    full_shape = values.shape
    leading = full_shape[:-1]
    reshaped = values.reshape(leading + (full_shape[-1] // (2 * pair_span), 2, pair_span))
    return jnp.flip(reshaped, axis=-2).reshape(full_shape)


def mix_local(matrices, current, partner, phase_row):
    own_term = jnp.dot(matrices[0], current, preferred_element_type=jnp.float32)
    partner_term = jnp.dot(matrices[1], partner, preferred_element_type=jnp.float32)
    return (jnp.cos(phase_row)[None] * own_term + jnp.sin(phase_row)[None] * partner_term).astype(
        jnp.bfloat16
    )


def plain_shards(source_field, project_mats, local_mats, cross_mats, angles, evaluate_mats):
    box_count = lax.axis_size("box")
    local_boxes = source_field.shape[1]
    rank_dim = project_mats.shape[0]
    pixel_rows = evaluate_mats.shape[0]
    local_levels = local_mats.shape[0]
    cross_levels = cross_mats.shape[0]
    group_size = local_boxes // box_count
    local_bits = (local_boxes & -local_boxes).bit_length() - 1
    box_bits = box_count.bit_length() - 1
    phases = angles.astype(jnp.float32)
    current = jnp.dot(project_mats, source_field, preferred_element_type=jnp.float32).astype(
        jnp.bfloat16
    )
    for level_idx in range(local_levels):
        partner = flip_last(current, 1 << level_idx % local_bits)
        current = mix_local(local_mats[level_idx], current, partner, phases[level_idx])
    for level_idx in range(cross_levels):
        level_bit = (box_bits - 1 - level_idx) % box_bits
        partner = swapped(current, "box", level_bit)
        current = mix_local(
            cross_mats[level_idx], current, partner, phases[local_levels + level_idx]
        )
    shaped = current.reshape(rank_dim, box_count, group_size)
    pixels_out = jnp.einsum(
        "qr,rdt->qdt",
        evaluate_mats,
        lax.all_to_all(shaped, "box", split_axis=1, concat_axis=1, tiled=True),
        preferred_element_type=jnp.float32,
    )
    return pixels_out.reshape(pixel_rows, local_boxes).astype(jnp.bfloat16)


def xor(a, b, bits):
    out = 0
    for i in range(bits):
        out = out + lax.rem(a // (1 << i) + b // (1 << i), 2) * (1 << i)
    return out


def cos_sin(t):
    u = t * 0.5
    w = u * u
    s = -1.0 / 39916800
    for coef in (1.0 / 362880, -1.0 / 5040, 1.0 / 120, -1.0 / 6, 1.0):
        s = s * w + coef
    s = s * u
    c = 1.0 / 479001600
    for coef in (-1.0 / 3628800, 1.0 / 40320, -1.0 / 720, 1.0 / 24, -0.5, 1.0):
        c = c * w + coef
    return 1.0 - 2.0 * s * s, 2.0 * s * c


def mix(matrix, own, partner, cos, sin):
    stacked = jnp.concatenate([(cos * own).astype(BF16), (sin * partner).astype(BF16)], axis=0)
    return jnp.dot(matrix, stacked, preferred_element_type=F32)


def lane_partner(x, span):
    lo, hi = x[:, :LANES], x[:, LANES:]
    if span == LANES:
        return jnp.concatenate([hi, lo], axis=1)
    index = lax.broadcasted_iota(jnp.int32, lo.shape, 1)
    index = jnp.bitwise_xor(index, span)
    parts = [jnp.take_along_axis(p, index, axis=1, mode="promise_in_bounds") for p in (lo, hi)]
    return jnp.concatenate(parts, axis=1)


def kernel(
    n_box, src_ref, proj_ref, local_ref, cross_ref, ang_ref, eval_ref, out_ref,
    snd, rcv, aux, ang_out, phase, local_w, s_snd, s_rcv, w_snd, w_rcv, a_snd, a_rcv, q_snd, q_rcv,
):
    bits = n_box.bit_length() - 1
    n_local, n_cross = local_ref.shape[0], cross_ref.shape[0]
    rank = proj_ref.shape[0]
    n_sub = rank // TILE
    group = src_ref.shape[1] // n_box
    w_rows = n_cross * TILE
    me = lax.axis_index("box")
    part = lax.axis_index("src")

    def peer(d):
        return xor(me, d, bits)

    def to_box(d):
        return (peer(d), part)

    part_y, part_c = xor(part, 2, 2), xor(part, 1, 2)
    barrier = pltpu.get_barrier_semaphore()
    for target in [to_box(d) for d in range(1, n_box)] + [(me, part_y), (me, part_c)]:
        pl.semaphore_signal(barrier, inc=1, device_id=target, device_id_type=MESH)

    for m in range(n_cross):
        rows = pl.ds(pl.multiple_of(part * TILE, TILE), TILE)
        aux[part, me, m * TILE:(m + 1) * TILE, :] = jnp.concatenate(
            [cross_ref[m, 0, rows, :], cross_ref[m, 1, rows, :]], axis=1
        )
    for l in range(n_local):
        local_w[l] = jnp.concatenate([local_ref[l, 0], local_ref[l, 1]], axis=1)
    phase[...] = jnp.zeros_like(phase)
    phase[0:n_local + n_cross, :] = ang_ref[...].astype(F32)

    def angle_tile(d):
        start = pl.multiple_of(peer(d) * group + part * UNIT, UNIT)
        block = phase[n_local:n_local + 8, pl.ds(start, UNIT)]
        return jnp.concatenate([block[:, :LANES], block[:, LANES:]], axis=0).astype(BF16)

    aux[part, me, w_rows:w_rows + TILE, :] = angle_tile(0)
    for d in range(1, n_box):
        ang_out[d] = angle_tile(d)

    def w_copy(d):
        low = d & -d
        piece = aux.at[part, peer(d - low), 0:w_rows]
        return pltpu.make_async_remote_copy(
            src_ref=piece, dst_ref=piece, send_sem=w_snd.at[d], recv_sem=w_rcv.at[d],
            device_id=to_box(low), device_id_type=MESH,
        )

    def a_copy(d):
        return pltpu.make_async_remote_copy(
            src_ref=ang_out.at[d], dst_ref=aux.at[part, me, w_rows:w_rows + TILE],
            send_sem=a_snd.at[d], recv_sem=a_rcv.at[d],
            device_id=to_box(d), device_id_type=MESH,
        )

    def q_copy(i):
        quarter = part if i < 2 else part_y
        return pltpu.make_async_remote_copy(
            src_ref=aux.at[quarter], dst_ref=aux.at[quarter],
            send_sem=q_snd.at[i], recv_sem=q_rcv.at[i],
            device_id=(me, part_y if i == 0 else part_c), device_id_type=MESH,
        )

    def s_copy(sub, d):
        return pltpu.make_async_remote_copy(
            src_ref=snd.at[sub, d], dst_ref=rcv.at[sub, me],
            send_sem=s_snd.at[sub, d], recv_sem=s_rcv.at[sub, d],
            device_id=to_box(d), device_id_type=MESH,
        )

    waves = [[d for d in range(1, n_box) if d & -d == 1 << i] for i in range(bits - 1, -1, -1)]

    pl.semaphore_wait(barrier, n_box + 1)
    for d in waves[0]:
        w_copy(d).start()
    for d in range(n_box - 1, 0, -1):
        a_copy(d).start()

    half_boxes = n_box // 2

    def local_step(it, carry):
        sub, half = it // 2, lax.rem(it, 2)
        first = half_boxes * (1 - half)
        xs, cs, ss = [], [], []
        for j in range(half_boxes):
            start = pl.multiple_of(peer(first + j) * group + sub * UNIT, UNIT)
            cols = pl.ds(start, UNIT)
            xs.append(jnp.dot(proj_ref[...], src_ref[:, cols], preferred_element_type=F32))
            cos, sin = cos_sin(phase[0:n_local, cols])
            cs.append(cos)
            ss.append(sin)
        for l in range(n_local):
            matrix = local_w[l]
            for j in range(half_boxes):
                x = xs[j]
                xs[j] = mix(matrix, x, lane_partner(x, 1 << l), cs[j][l:l + 1], ss[j][l:l + 1])
        for j in range(half_boxes):
            snd[sub, first + j] = xs[j].astype(BF16)
        for j in range(1, half_boxes):
            s_copy(sub, first + j).start()

        @pl.when(half == 0)
        def _():
            s_copy(sub, first).start()

        @pl.when(half == 1)
        def _():
            rcv[sub, me] = xs[0].astype(BF16)

        for i in range(1, bits):
            @pl.when(it == i)
            def _(i=i):
                for d in waves[i - 1]:
                    w_copy(d).wait_recv()
                for d in waves[i]:
                    w_copy(d).start()

        @pl.when(it == bits + 1)
        def _():
            for d in waves[-1]:
                w_copy(d).wait_recv()
            for d in range(1, n_box):
                a_copy(d).wait_recv()
            q_copy(0).start()
            q_copy(1).start()

        @pl.when(it == bits + 3)
        def _():
            q_copy(0).wait_recv()
            q_copy(2).start()

        return carry

    lax.fori_loop(0, 2 * n_sub, local_step, 0)
    q_copy(1).wait_recv()
    q_copy(2).wait_recv()

    def cross_step(sub, carry):
        for d in range(1, n_box):
            s_copy(sub, d).wait_recv()
        xs = [rcv[sub, k].astype(F32) for k in range(n_box)]
        tables = [cos_sin(aux[sub, k, w_rows:w_rows + TILE, :].astype(F32)) for k in range(n_box)]

        def row(table, m):
            return jnp.concatenate([table[m:m + 1], table[8 + m:9 + m]], axis=1)

        for m in range(n_cross):
            bit = 1 << (bits - 1 - m) % bits
            new = []
            for k in range(n_box):
                matrix = jnp.concatenate(
                    [aux[q, k, m * TILE:(m + 1) * TILE, :] for q in range(n_sub)], axis=0
                )
                cos, sin = tables[k]
                new.append(mix(matrix, xs[k], xs[k ^ bit], row(cos, m), row(sin, m)))
            xs = new
        for k in range(n_box):
            pixels = jnp.dot(eval_ref[...], xs[k].astype(BF16), preferred_element_type=F32)
            start = pl.multiple_of(k * group + sub * UNIT, UNIT)
            out_ref[:, pl.ds(start, UNIT)] = pixels.astype(BF16)
        return carry

    lax.fori_loop(0, n_sub, cross_step, 0)

    def drain(sub, carry):
        for d in range(1, n_box):
            s_copy(sub, d).wait_send()
        return carry

    lax.fori_loop(0, n_sub, drain, 0)
    for d in range(1, n_box):
        w_copy(d).wait_send()
        a_copy(d).wait_send()
    for i in range(3):
        q_copy(i).wait_send()


def shards(source_field, project_mats, local_mats, cross_mats, angles, evaluate_mats):
    n_box = lax.axis_size("box")
    rank = project_mats.shape[0]
    n_sub = rank // TILE
    n_cross = cross_mats.shape[0]
    boxes = source_field.shape[1]
    pixels = evaluate_mats.shape[0]
    rows = n_cross * TILE + TILE
    dma = pltpu.SemaphoreType.DMA
    flops = 2 * boxes * rank * (2 * pixels + 2 * rank * angles.shape[0])
    return pl.pallas_call(
        functools.partial(kernel, n_box),
        out_shape=jax.ShapeDtypeStruct((pixels, boxes), BF16),
        in_specs=[pl.BlockSpec(memory_space=pltpu.VMEM)] * 6,
        out_specs=pl.BlockSpec(memory_space=pltpu.VMEM),
        scratch_shapes=[
            pltpu.VMEM((n_sub, n_box, rank, UNIT), BF16),
            pltpu.VMEM((n_sub, n_box, rank, UNIT), BF16),
            pltpu.VMEM((n_sub, n_box, rows, LANES), BF16),
            pltpu.VMEM((n_box, TILE, LANES), BF16),
            pltpu.VMEM((2 * 8, boxes), F32),
            pltpu.VMEM((local_mats.shape[0], rank, 2 * rank), BF16),
            dma((n_sub, n_box)), dma((n_sub, n_box)),
            dma((n_box,)), dma((n_box,)),
            dma((n_box,)), dma((n_box,)),
            dma((3,)), dma((3,)),
        ],
        compiler_params=pltpu.CompilerParams(
            collective_id=0, has_side_effects=True, vmem_limit_bytes=48 * 1024 * 1024
        ),
        cost_estimate=pl.CostEstimate(
            flops=flops, bytes_accessed=4 * boxes * pixels, transcendentals=0
        ),
    )(source_field, project_mats, local_mats, cross_mats, angles, evaluate_mats)


def fits_kernel(mesh):
    return mesh.shape["box"] == 8 and mesh.shape["src"] == 4


def solution(mesh):
    in_specs = (
        P("src", "box"),
        P("box", None),
        P(None, None, "box", None),
        P(None, None, "box", None),
        P(None, "box"),
        P("box", None),
    )
    out_specs = P("src", "box")
    body = shards if fits_kernel(mesh) else plain_shards
    return jax.shard_map(body, mesh=mesh, in_specs=in_specs, out_specs=out_specs, check_vma=False)
```

```python
import functools

import jax
import jax.numpy as jnp
from jax import lax
from jax.experimental import pallas as pl
from jax.experimental.pallas import tpu as pltpu
from jax.sharding import PartitionSpec as P

MESH = pl.DeviceIdType.MESH
F32 = jnp.float32
BF16 = jnp.bfloat16
LANES = 128
TILE = 16
UNIT = 256


def swapped(x, axis, distance):
    return lax.ppermute(x, axis, [(i, i ^ 1 << distance) for i in range(lax.axis_size(axis))])


def flip_last(values, pair_span):
    full_shape = values.shape
    leading = full_shape[:-1]
    reshaped = values.reshape(leading + (full_shape[-1] // (2 * pair_span), 2, pair_span))
    return jnp.flip(reshaped, axis=-2).reshape(full_shape)


def mix_local(matrices, current, partner, phase_row):
    own_term = jnp.dot(matrices[0], current, preferred_element_type=jnp.float32)
    partner_term = jnp.dot(matrices[1], partner, preferred_element_type=jnp.float32)
    return (jnp.cos(phase_row)[None] * own_term + jnp.sin(phase_row)[None] * partner_term).astype(
        jnp.bfloat16
    )


def plain_shards(source_field, project_mats, local_mats, cross_mats, angles, evaluate_mats):
    box_count = lax.axis_size("box")
    local_boxes = source_field.shape[1]
    rank_dim = project_mats.shape[0]
    pixel_rows = evaluate_mats.shape[0]
    local_levels = local_mats.shape[0]
    cross_levels = cross_mats.shape[0]
    group_size = local_boxes // box_count
    local_bits = (local_boxes & -local_boxes).bit_length() - 1
    box_bits = box_count.bit_length() - 1
    phases = angles.astype(jnp.float32)
    current = jnp.dot(project_mats, source_field, preferred_element_type=jnp.float32).astype(
        jnp.bfloat16
    )
    for level_idx in range(local_levels):
        partner = flip_last(current, 1 << level_idx % local_bits)
        current = mix_local(local_mats[level_idx], current, partner, phases[level_idx])
    for level_idx in range(cross_levels):
        level_bit = (box_bits - 1 - level_idx) % box_bits
        partner = swapped(current, "box", level_bit)
        current = mix_local(
            cross_mats[level_idx], current, partner, phases[local_levels + level_idx]
        )
    shaped = current.reshape(rank_dim, box_count, group_size)
    pixels_out = jnp.einsum(
        "qr,rdt->qdt",
        evaluate_mats,
        lax.all_to_all(shaped, "box", split_axis=1, concat_axis=1, tiled=True),
        preferred_element_type=jnp.float32,
    )
    return pixels_out.reshape(pixel_rows, local_boxes).astype(jnp.bfloat16)


def xor(a, b, bits):
    out = 0
    for i in range(bits):
        out = out + lax.rem(a // (1 << i) + b // (1 << i), 2) * (1 << i)
    return out


def cos_sin(t):
    u = t * 0.5
    w = u * u
    s = -1.0 / 39916800
    for coef in (1.0 / 362880, -1.0 / 5040, 1.0 / 120, -1.0 / 6, 1.0):
        s = s * w + coef
    s = s * u
    c = 1.0 / 479001600
    for coef in (-1.0 / 3628800, 1.0 / 40320, -1.0 / 720, 1.0 / 24, -0.5, 1.0):
        c = c * w + coef
    return 1.0 - 2.0 * s * s, 2.0 * s * c


def mix(matrix, own, partner, cos, sin):
    stacked = jnp.concatenate([(cos * own).astype(BF16), (sin * partner).astype(BF16)], axis=0)
    return jnp.dot(matrix, stacked, preferred_element_type=F32)


def lane_partner(x, span):
    lo, hi = x[:, :LANES], x[:, LANES:]
    if span == LANES:
        return jnp.concatenate([hi, lo], axis=1)
    index = lax.broadcasted_iota(jnp.int32, lo.shape, 1)
    index = jnp.bitwise_xor(index, span)
    parts = [jnp.take_along_axis(p, index, axis=1, mode="promise_in_bounds") for p in (lo, hi)]
    return jnp.concatenate(parts, axis=1)


def kernel(
    n_box, src_hbm, proj_hbm, local_hbm, cross_hbm, ang_hbm, eval_hbm, out_hbm,
    src_ref, proj_ref, local_ref, cross_ref, ang_ref, eval_t_ref, eval_ref,
    snd, rcv, aux, ang_out, local_w, out_ref, in_sem, src_sem, out_sem,
    s_snd, s_rcv, w_snd, w_rcv, a_snd, a_rcv, q_snd, q_rcv,
):
    bits = n_box.bit_length() - 1
    n_local, n_cross = local_ref.shape[0], cross_ref.shape[0]
    rank = proj_ref.shape[0]
    n_sub = rank // TILE
    group = src_hbm.shape[1] // n_box
    w_rows = n_cross * TILE
    me = lax.axis_index("box")
    part = lax.axis_index("src")

    def peer(d):
        return xor(me, d, bits)

    def to_box(d):
        return (peer(d), part)

    part_y, part_c = xor(part, 2, 2), xor(part, 1, 2)
    barrier = pltpu.get_barrier_semaphore()
    for target in [to_box(d) for d in range(1, n_box)] + [(me, part_y), (me, part_c)]:
        pl.semaphore_signal(barrier, inc=1, device_id=target, device_id_type=MESH)

    def load(i, source, target):
        return pltpu.make_async_copy(source, target, in_sem.at[i])

    loads = [
        load(i, *pair)
        for i, pair in enumerate([
            (proj_hbm, proj_ref), (ang_hbm, ang_ref), (local_hbm, local_ref),
            (cross_hbm, cross_ref), (eval_hbm, eval_t_ref),
        ])
    ]

    def columns(sub, d):
        return pl.ds(pl.multiple_of(peer(d) * group + sub * UNIT, UNIT), UNIT)

    def load_source(sub, d):
        return pltpu.make_async_copy(
            src_hbm.at[:, columns(sub, d)], src_ref.at[sub, d], src_sem.at[sub, d]
        )

    def start_unit(it):
        for j in range(half_boxes):
            load_source(it // 2, half_boxes * (1 - lax.rem(it, 2)) + j).start()

    half_boxes = n_box // 2
    for copy in loads[:3]:
        copy.start()
    start_unit(0)
    for copy in loads[3:]:
        copy.start()

    def start_rest(it, carry):
        start_unit(it)
        return carry

    lax.fori_loop(1, 2 * n_sub, start_rest, 0)
    for copy in loads[:3]:
        copy.wait()
    for l in range(n_local):
        local_w[l] = jnp.concatenate([local_ref[l, 0], local_ref[l, 1]], axis=1)

    def angle_tile(d):
        block = ang_ref[:, columns(part, d)].astype(F32)[n_local:n_local + n_cross]
        block = jnp.concatenate([block, jnp.zeros((8 - n_cross, UNIT), F32)], axis=0)
        return jnp.concatenate([block[:, :LANES], block[:, LANES:]], axis=0).astype(BF16)

    def prepare_aux():
        for copy in loads[3:]:
            copy.wait()
        for m in range(n_cross):
            rows = pl.ds(pl.multiple_of(part * TILE, TILE), TILE)
            aux[part, me, m * TILE:(m + 1) * TILE, :] = jnp.concatenate(
                [cross_ref[m, 0, rows, :], cross_ref[m, 1, rows, :]], axis=1
            )
        aux[part, me, w_rows:w_rows + TILE, :] = angle_tile(0)
        for d in range(1, n_box):
            ang_out[d] = angle_tile(d)
        eval_ref[...] = eval_t_ref[...].astype(F32).T.astype(BF16)

    def w_copy(d):
        low = d & -d
        piece = aux.at[part, peer(d - low), 0:w_rows]
        return pltpu.make_async_remote_copy(
            src_ref=piece, dst_ref=piece, send_sem=w_snd.at[d], recv_sem=w_rcv.at[d],
            device_id=to_box(low), device_id_type=MESH,
        )

    def a_copy(d):
        return pltpu.make_async_remote_copy(
            src_ref=ang_out.at[d], dst_ref=aux.at[part, me, w_rows:w_rows + TILE],
            send_sem=a_snd.at[d], recv_sem=a_rcv.at[d],
            device_id=to_box(d), device_id_type=MESH,
        )

    def q_copy(i):
        quarter = part if i < 2 else part_y
        return pltpu.make_async_remote_copy(
            src_ref=aux.at[quarter], dst_ref=aux.at[quarter],
            send_sem=q_snd.at[i], recv_sem=q_rcv.at[i],
            device_id=(me, part_y if i == 0 else part_c), device_id_type=MESH,
        )

    def s_copy(sub, d):
        return pltpu.make_async_remote_copy(
            src_ref=snd.at[sub, d], dst_ref=rcv.at[sub, me],
            send_sem=s_snd.at[sub, d], recv_sem=s_rcv.at[sub, d],
            device_id=to_box(d), device_id_type=MESH,
        )

    waves = [[d for d in range(1, n_box) if d & -d == 1 << i] for i in range(bits - 1, -1, -1)]

    def local_step(it, carry):
        sub, half = it // 2, lax.rem(it, 2)
        first = half_boxes * (1 - half)
        xs, cs, ss = [], [], []
        for j in range(half_boxes):
            load_source(sub, first + j).wait()
            xs.append(
                jnp.dot(proj_ref[...], src_ref[sub, first + j], preferred_element_type=F32)
            )
            cos, sin = cos_sin(ang_ref[:, columns(sub, first + j)].astype(F32)[:n_local])
            cs.append(cos)
            ss.append(sin)
        for l in range(n_local):
            matrix = local_w[l]
            for j in range(half_boxes):
                x = xs[j]
                xs[j] = mix(matrix, x, lane_partner(x, 1 << l), cs[j][l:l + 1], ss[j][l:l + 1])
        for j in range(half_boxes):
            snd[sub, first + j] = xs[j].astype(BF16)

        @pl.when(it == 0)
        def _():
            pl.semaphore_wait(barrier, n_box + 1)

        for j in range(1, half_boxes):
            s_copy(sub, first + j).start()

        @pl.when(half == 0)
        def _():
            s_copy(sub, first).start()

        @pl.when(half == 1)
        def _():
            rcv[sub, me] = xs[0].astype(BF16)

        @pl.when(it == 0)
        def _():
            prepare_aux()
            for d in waves[0]:
                w_copy(d).start()
            for d in range(n_box - 1, 0, -1):
                a_copy(d).start()

        for i in range(1, bits):
            @pl.when(it == i)
            def _(i=i):
                for d in waves[i - 1]:
                    w_copy(d).wait_recv()
                for d in waves[i]:
                    w_copy(d).start()

        @pl.when(it == bits + 1)
        def _():
            for d in waves[-1]:
                w_copy(d).wait_recv()
            for d in range(1, n_box):
                a_copy(d).wait_recv()
            q_copy(0).start()
            q_copy(1).start()

        @pl.when(it == bits + 3)
        def _():
            q_copy(0).wait_recv()
            q_copy(2).start()

        return carry

    lax.fori_loop(0, 2 * n_sub, local_step, 0)
    q_copy(1).wait_recv()
    q_copy(2).wait_recv()

    def store(sub, k):
        start = pl.multiple_of(k * group + sub * UNIT, UNIT)
        return pltpu.make_async_copy(
            out_ref.at[sub, k], out_hbm.at[:, pl.ds(start, UNIT)], out_sem.at[sub, k]
        )

    def cross_step(sub, carry):
        for d in range(1, n_box):
            s_copy(sub, d).wait_recv()
        xs = [rcv[sub, k].astype(F32) for k in range(n_box)]
        tables = [cos_sin(aux[sub, k, w_rows:w_rows + TILE, :].astype(F32)) for k in range(n_box)]

        def row(table, m):
            return jnp.concatenate([table[m:m + 1], table[8 + m:9 + m]], axis=1)

        for m in range(n_cross):
            bit = 1 << (bits - 1 - m) % bits
            new = []
            for k in range(n_box):
                matrix = jnp.concatenate(
                    [aux[q, k, m * TILE:(m + 1) * TILE, :] for q in range(n_sub)], axis=0
                )
                cos, sin = tables[k]
                new.append(mix(matrix, xs[k], xs[k ^ bit], row(cos, m), row(sin, m)))
            xs = new
        for k in range(n_box):
            pixels = jnp.dot(eval_ref[...], xs[k].astype(BF16), preferred_element_type=F32)
            out_ref[sub, k] = pixels.astype(BF16)
            store(sub, k).start()
        return carry

    lax.fori_loop(0, n_sub, cross_step, 0)

    def drain(sub, carry):
        for d in range(1, n_box):
            s_copy(sub, d).wait_send()
        for k in range(n_box):
            store(sub, k).wait()
        return carry

    lax.fori_loop(0, n_sub, drain, 0)
    for d in range(1, n_box):
        w_copy(d).wait_send()
        a_copy(d).wait_send()
    for i in range(3):
        q_copy(i).wait_send()


def shards(source_field, project_mats, local_mats, cross_mats, angles, evaluate_mats):
    n_box = lax.axis_size("box")
    rank = project_mats.shape[0]
    n_sub = rank // TILE
    n_cross = cross_mats.shape[0]
    boxes = source_field.shape[1]
    pixels = evaluate_mats.shape[0]
    rows = n_cross * TILE + TILE
    dma = pltpu.SemaphoreType.DMA
    flops = 2 * boxes * rank * (2 * pixels + 2 * rank * angles.shape[0])
    return pl.pallas_call(
        functools.partial(kernel, n_box),
        out_shape=jax.ShapeDtypeStruct((pixels, boxes), BF16),
        in_specs=[pl.BlockSpec(memory_space=pltpu.HBM)] * 6,
        out_specs=pl.BlockSpec(memory_space=pltpu.HBM),
        scratch_shapes=[
            pltpu.VMEM((n_sub, n_box, pixels, UNIT), BF16),
            pltpu.VMEM(project_mats.shape, BF16),
            pltpu.VMEM(local_mats.shape, BF16),
            pltpu.VMEM(cross_mats.shape, BF16),
            pltpu.VMEM(angles.shape, BF16),
            pltpu.VMEM((rank, pixels), BF16),
            pltpu.VMEM((pixels, rank), BF16),
            pltpu.VMEM((n_sub, n_box, rank, UNIT), BF16),
            pltpu.VMEM((n_sub, n_box, rank, UNIT), BF16),
            pltpu.VMEM((n_sub, n_box, rows, LANES), BF16),
            pltpu.VMEM((n_box, TILE, LANES), BF16),
            pltpu.VMEM((local_mats.shape[0], rank, 2 * rank), BF16),
            pltpu.VMEM((n_sub, n_box, pixels, UNIT), BF16),
            dma((5,)), dma((n_sub, n_box)), dma((n_sub, n_box)),
            dma((n_sub, n_box)), dma((n_sub, n_box)),
            dma((n_box,)), dma((n_box,)),
            dma((n_box,)), dma((n_box,)),
            dma((3,)), dma((3,)),
        ],
        compiler_params=pltpu.CompilerParams(
            collective_id=0, has_side_effects=True, vmem_limit_bytes=60 * 1024 * 1024
        ),
        cost_estimate=pl.CostEstimate(
            flops=flops, bytes_accessed=4 * boxes * pixels, transcendentals=0
        ),
    )(source_field, project_mats, local_mats, cross_mats, angles, evaluate_mats.T)


def fits_kernel(mesh):
    return mesh.shape["box"] == 8 and mesh.shape["src"] == 4


def solution(mesh):
    in_specs = (
        P("src", "box"),
        P("box", None),
        P(None, None, "box", None),
        P(None, None, "box", None),
        P(None, "box"),
        P("box", None),
    )
    out_specs = P("src", "box")
    body = shards if fits_kernel(mesh) else plain_shards
    return jax.shard_map(body, mesh=mesh, in_specs=in_specs, out_specs=out_specs, check_vma=False)
```

```python
import functools

import jax
import jax.numpy as jnp
from jax import lax
from jax.experimental import pallas as pl
from jax.experimental.pallas import tpu as pltpu
from jax.sharding import PartitionSpec as P

MESH = pl.DeviceIdType.MESH
F32 = jnp.float32
BF16 = jnp.bfloat16
LANES = 128
TILE = 16
UNIT = 256


def swapped(x, axis, distance):
    return lax.ppermute(x, axis, [(i, i ^ 1 << distance) for i in range(lax.axis_size(axis))])


def flip_last(values, pair_span):
    full_shape = values.shape
    leading = full_shape[:-1]
    reshaped = values.reshape(leading + (full_shape[-1] // (2 * pair_span), 2, pair_span))
    return jnp.flip(reshaped, axis=-2).reshape(full_shape)


def mix_local(matrices, current, partner, phase_row):
    own_term = jnp.dot(matrices[0], current, preferred_element_type=jnp.float32)
    partner_term = jnp.dot(matrices[1], partner, preferred_element_type=jnp.float32)
    return (jnp.cos(phase_row)[None] * own_term + jnp.sin(phase_row)[None] * partner_term).astype(
        jnp.bfloat16
    )


def plain_shards(source_field, project_mats, local_mats, cross_mats, angles, evaluate_mats):
    box_count = lax.axis_size("box")
    local_boxes = source_field.shape[1]
    rank_dim = project_mats.shape[0]
    pixel_rows = evaluate_mats.shape[0]
    local_levels = local_mats.shape[0]
    cross_levels = cross_mats.shape[0]
    group_size = local_boxes // box_count
    local_bits = (local_boxes & -local_boxes).bit_length() - 1
    box_bits = box_count.bit_length() - 1
    phases = angles.astype(jnp.float32)
    current = jnp.dot(project_mats, source_field, preferred_element_type=jnp.float32).astype(
        jnp.bfloat16
    )
    for level_idx in range(local_levels):
        partner = flip_last(current, 1 << level_idx % local_bits)
        current = mix_local(local_mats[level_idx], current, partner, phases[level_idx])
    for level_idx in range(cross_levels):
        level_bit = (box_bits - 1 - level_idx) % box_bits
        partner = swapped(current, "box", level_bit)
        current = mix_local(
            cross_mats[level_idx], current, partner, phases[local_levels + level_idx]
        )
    shaped = current.reshape(rank_dim, box_count, group_size)
    pixels_out = jnp.einsum(
        "qr,rdt->qdt",
        evaluate_mats,
        lax.all_to_all(shaped, "box", split_axis=1, concat_axis=1, tiled=True),
        preferred_element_type=jnp.float32,
    )
    return pixels_out.reshape(pixel_rows, local_boxes).astype(jnp.bfloat16)


def xor(a, b, bits):
    out = 0
    for i in range(bits):
        out = out + lax.rem(a // (1 << i) + b // (1 << i), 2) * (1 << i)
    return out


def cos_sin(t):
    u = t * 0.5
    w = u * u
    s = -1.0 / 39916800
    for coef in (1.0 / 362880, -1.0 / 5040, 1.0 / 120, -1.0 / 6, 1.0):
        s = s * w + coef
    s = s * u
    c = 1.0 / 479001600
    for coef in (-1.0 / 3628800, 1.0 / 40320, -1.0 / 720, 1.0 / 24, -0.5, 1.0):
        c = c * w + coef
    return 1.0 - 2.0 * s * s, 2.0 * s * c


def mix(matrix, own, partner, cos, sin):
    stacked = jnp.concatenate([(cos * own).astype(BF16), (sin * partner).astype(BF16)], axis=0)
    return jnp.dot(matrix, stacked, preferred_element_type=F32)


def lane_partner(x, span):
    lo, hi = x[:, :LANES], x[:, LANES:]
    if span == LANES:
        return jnp.concatenate([hi, lo], axis=1)
    index = lax.broadcasted_iota(jnp.int32, lo.shape, 1)
    index = jnp.bitwise_xor(index, span)
    parts = [jnp.take_along_axis(p, index, axis=1, mode="promise_in_bounds") for p in (lo, hi)]
    return jnp.concatenate(parts, axis=1)


def kernel(
    n_box, src_hbm, proj_hbm, local_hbm, cross_hbm, ang_hbm, eval_hbm, out_ref,
    src_ref, proj_ref, local_ref, cross_ref, ang_ref, eval_t_ref, eval_ref,
    snd, rcv, aux, ang_out, local_w, in_sem, src_sem,
    s_snd, s_rcv, w_snd, w_rcv, a_snd, a_rcv, q_snd, q_rcv,
):
    bits = n_box.bit_length() - 1
    n_local, n_cross = local_ref.shape[0], cross_ref.shape[0]
    rank = proj_ref.shape[0]
    n_sub = rank // TILE
    group = src_hbm.shape[1] // n_box
    w_rows = n_cross * TILE
    me = lax.axis_index("box")
    part = lax.axis_index("src")

    def peer(d):
        return xor(me, d, bits)

    def to_box(d):
        return (peer(d), part)

    part_y, part_c = xor(part, 2, 2), xor(part, 1, 2)
    barrier = pltpu.get_barrier_semaphore()
    for target in [to_box(d) for d in range(1, n_box)] + [(me, part_y), (me, part_c)]:
        pl.semaphore_signal(barrier, inc=1, device_id=target, device_id_type=MESH)

    def load(i, source, target):
        return pltpu.make_async_copy(source, target, in_sem.at[i])

    loads = [
        load(i, *pair)
        for i, pair in enumerate([
            (proj_hbm, proj_ref), (ang_hbm, ang_ref), (local_hbm, local_ref),
            (cross_hbm, cross_ref), (eval_hbm, eval_t_ref),
        ])
    ]

    def columns(sub, d):
        return pl.ds(pl.multiple_of(peer(d) * group + sub * UNIT, UNIT), UNIT)

    def load_source(sub, d):
        return pltpu.make_async_copy(
            src_hbm.at[:, columns(sub, d)], src_ref.at[sub, d], src_sem.at[sub, d]
        )

    far = n_box // 2
    order = list(range(far, n_box)) + list(range(far - 1, -1, -1))

    def start_unit(sub):
        for d in order:
            load_source(sub, d).start()

    for copy in loads[:3]:
        copy.start()
    start_unit(0)
    for copy in loads[3:]:
        copy.start()

    def start_rest(it, carry):
        start_unit(it)
        return carry

    lax.fori_loop(1, n_sub, start_rest, 0)
    for copy in loads[:3]:
        copy.wait()
    for l in range(n_local):
        local_w[l] = jnp.concatenate([local_ref[l, 0], local_ref[l, 1]], axis=1)

    def angle_tile(d):
        block = ang_ref[:, columns(part, d)].astype(F32)[n_local:n_local + n_cross]
        block = jnp.concatenate([block, jnp.zeros((8 - n_cross, UNIT), F32)], axis=0)
        return jnp.concatenate([block[:, :LANES], block[:, LANES:]], axis=0).astype(BF16)

    def prepare_aux():
        for copy in loads[3:]:
            copy.wait()
        for m in range(n_cross):
            rows = pl.ds(pl.multiple_of(part * TILE, TILE), TILE)
            aux[part, me, m * TILE:(m + 1) * TILE, :] = jnp.concatenate(
                [cross_ref[m, 0, rows, :], cross_ref[m, 1, rows, :]], axis=1
            )
        aux[part, me, w_rows:w_rows + TILE, :] = angle_tile(0)
        for d in range(1, n_box):
            ang_out[d] = angle_tile(d)
        eval_ref[...] = eval_t_ref[...].astype(F32).T.astype(BF16)

    def w_copy(d):
        low = d if d <= far else d - far
        piece = aux.at[part, peer(d - low), 0:w_rows]
        return pltpu.make_async_remote_copy(
            src_ref=piece, dst_ref=piece, send_sem=w_snd.at[d], recv_sem=w_rcv.at[d],
            device_id=to_box(low), device_id_type=MESH,
        )

    def a_copy(d):
        return pltpu.make_async_remote_copy(
            src_ref=ang_out.at[d], dst_ref=aux.at[part, me, w_rows:w_rows + TILE],
            send_sem=a_snd.at[d], recv_sem=a_rcv.at[d],
            device_id=to_box(d), device_id_type=MESH,
        )

    def q_copy(i):
        quarter = part if i < 2 else part_y
        return pltpu.make_async_remote_copy(
            src_ref=aux.at[quarter], dst_ref=aux.at[quarter],
            send_sem=q_snd.at[i], recv_sem=q_rcv.at[i],
            device_id=(me, part_y if i == 0 else part_c), device_id_type=MESH,
        )

    def s_copy(sub, d):
        return pltpu.make_async_remote_copy(
            src_ref=snd.at[sub, d], dst_ref=rcv.at[sub, me],
            send_sem=s_snd.at[sub, d], recv_sem=s_rcv.at[sub, d],
            device_id=to_box(d), device_id_type=MESH,
        )

    def local_step(sub, carry):
        xs, cs, ss = {}, {}, {}
        for d in order:
            load_source(sub, d).wait()
        for d in order:
            xs[d] = jnp.dot(proj_ref[...], src_ref[sub, d], preferred_element_type=F32)
            cs[d], ss[d] = cos_sin(ang_ref[:, columns(sub, d)].astype(F32)[:n_local])
        for l in range(n_local):
            if l == n_local // 2:
                @pl.when(sub == 0)
                def _():
                    pl.semaphore_wait(barrier, n_box + 1)

                @pl.when(sub == 1)
                def _():
                    w_copy(far).wait_recv()
                    for d in range(far + 1, n_box):
                        w_copy(d).start()

                @pl.when(sub == n_sub - 1)
                def _():
                    q_copy(0).wait_recv()
                    q_copy(2).start()

            matrix = local_w[l]
            for d in order:
                x = xs[d]
                xs[d] = mix(matrix, x, lane_partner(x, 1 << l), cs[d][l:l + 1], ss[d][l:l + 1])
        for d in order:
            snd[sub, d] = xs[d].astype(BF16)

        for d in order:
            if d:
                s_copy(sub, d).start()
            else:
                rcv[sub, me] = xs[0].astype(BF16)

        @pl.when(sub == 0)
        def _():
            prepare_aux()
            for d in range(far, 0, -1):
                w_copy(d).start()
            for d in range(n_box - 1, 0, -1):
                a_copy(d).start()

        @pl.when(sub == 1)
        def _():
            for d in range(1, n_box):
                if d != far:
                    w_copy(d).wait_recv()
                a_copy(d).wait_recv()
            q_copy(0).start()
            q_copy(1).start()

        return carry

    lax.fori_loop(0, n_sub, local_step, 0)
    q_copy(1).wait_recv()
    q_copy(2).wait_recv()

    def cross_step(sub, carry):
        for d in range(1, n_box):
            s_copy(sub, d).wait_recv()
        xs = [rcv[sub, k].astype(F32) for k in range(n_box)]
        tables = [cos_sin(aux[sub, k, w_rows:w_rows + TILE, :].astype(F32)) for k in range(n_box)]

        def row(table, m):
            return jnp.concatenate([table[m:m + 1], table[8 + m:9 + m]], axis=1)

        for m in range(n_cross):
            bit = 1 << (bits - 1 - m) % bits
            new = []
            for k in range(n_box):
                matrix = jnp.concatenate(
                    [aux[q, k, m * TILE:(m + 1) * TILE, :] for q in range(n_sub)], axis=0
                )
                cos, sin = tables[k]
                new.append(mix(matrix, xs[k], xs[k ^ bit], row(cos, m), row(sin, m)))
            xs = new
        for k in range(n_box):
            pixels = jnp.dot(eval_ref[...], xs[k].astype(BF16), preferred_element_type=F32)
            start = pl.multiple_of(k * group + sub * UNIT, UNIT)
            out_ref[:, pl.ds(start, UNIT)] = pixels.astype(BF16)
        return carry

    lax.fori_loop(0, n_sub, cross_step, 0)

    def drain(sub, carry):
        for d in range(1, n_box):
            s_copy(sub, d).wait_send()
        return carry

    lax.fori_loop(0, n_sub, drain, 0)
    for d in range(1, n_box):
        w_copy(d).wait_send()
        a_copy(d).wait_send()
    for i in range(3):
        q_copy(i).wait_send()


def shards(source_field, project_mats, local_mats, cross_mats, angles, evaluate_mats):
    n_box = lax.axis_size("box")
    rank = project_mats.shape[0]
    n_sub = rank // TILE
    n_cross = cross_mats.shape[0]
    boxes = source_field.shape[1]
    pixels = evaluate_mats.shape[0]
    rows = n_cross * TILE + TILE
    dma = pltpu.SemaphoreType.DMA
    flops = 2 * boxes * rank * (2 * pixels + 2 * rank * angles.shape[0])
    return pl.pallas_call(
        functools.partial(kernel, n_box),
        out_shape=pltpu.VMEM((pixels, boxes), BF16),
        in_specs=[pl.BlockSpec(memory_space=pltpu.HBM)] * 6,
        out_specs=pl.BlockSpec(memory_space=pltpu.VMEM),
        scratch_shapes=[
            pltpu.VMEM((n_sub, n_box, pixels, UNIT), BF16),
            pltpu.VMEM(project_mats.shape, BF16),
            pltpu.VMEM(local_mats.shape, BF16),
            pltpu.VMEM(cross_mats.shape, BF16),
            pltpu.VMEM(angles.shape, BF16),
            pltpu.VMEM((rank, pixels), BF16),
            pltpu.VMEM((pixels, rank), BF16),
            pltpu.VMEM((n_sub, n_box, rank, UNIT), BF16),
            pltpu.VMEM((n_sub, n_box, rank, UNIT), BF16),
            pltpu.VMEM((n_sub, n_box, rows, LANES), BF16),
            pltpu.VMEM((n_box, TILE, LANES), BF16),
            pltpu.VMEM((local_mats.shape[0], rank, 2 * rank), BF16),
            dma((5,)), dma((n_sub, n_box)),
            dma((n_sub, n_box)), dma((n_sub, n_box)),
            dma((n_box,)), dma((n_box,)),
            dma((n_box,)), dma((n_box,)),
            dma((3,)), dma((3,)),
        ],
        compiler_params=pltpu.CompilerParams(
            collective_id=0, has_side_effects=True, vmem_limit_bytes=60 * 1024 * 1024
        ),
        cost_estimate=pl.CostEstimate(
            flops=flops, bytes_accessed=4 * boxes * pixels, transcendentals=0
        ),
    )(source_field, project_mats, local_mats, cross_mats, angles, evaluate_mats.T)


def fits_kernel(mesh):
    return mesh.shape["box"] == 8 and mesh.shape["src"] == 4


def solution(mesh):
    in_specs = (
        P("src", "box"),
        P("box", None),
        P(None, None, "box", None),
        P(None, None, "box", None),
        P(None, "box"),
        P("box", None),
    )
    out_specs = P("src", "box")
    body = shards if fits_kernel(mesh) else plain_shards
    return jax.shard_map(body, mesh=mesh, in_specs=in_specs, out_specs=out_specs, check_vma=False)
```

```python
import functools

import jax
import jax.numpy as jnp
from jax import lax
from jax.experimental import pallas as pl
from jax.experimental.pallas import tpu as pltpu
from jax.sharding import PartitionSpec as P

MESH = pl.DeviceIdType.MESH
F32 = jnp.float32
BF16 = jnp.bfloat16
LANES = 128
TILE = 16
UNIT = 256


def swapped(x, axis, distance):
    return lax.ppermute(x, axis, [(i, i ^ 1 << distance) for i in range(lax.axis_size(axis))])


def flip_last(values, pair_span):
    full_shape = values.shape
    leading = full_shape[:-1]
    reshaped = values.reshape(leading + (full_shape[-1] // (2 * pair_span), 2, pair_span))
    return jnp.flip(reshaped, axis=-2).reshape(full_shape)


def mix_local(matrices, current, partner, phase_row):
    own_term = jnp.dot(matrices[0], current, preferred_element_type=jnp.float32)
    partner_term = jnp.dot(matrices[1], partner, preferred_element_type=jnp.float32)
    return (jnp.cos(phase_row)[None] * own_term + jnp.sin(phase_row)[None] * partner_term).astype(
        jnp.bfloat16
    )


def plain_shards(source_field, project_mats, local_mats, cross_mats, angles, evaluate_mats):
    box_count = lax.axis_size("box")
    local_boxes = source_field.shape[1]
    rank_dim = project_mats.shape[0]
    pixel_rows = evaluate_mats.shape[0]
    local_levels = local_mats.shape[0]
    cross_levels = cross_mats.shape[0]
    group_size = local_boxes // box_count
    local_bits = (local_boxes & -local_boxes).bit_length() - 1
    box_bits = box_count.bit_length() - 1
    phases = angles.astype(jnp.float32)
    current = jnp.dot(project_mats, source_field, preferred_element_type=jnp.float32).astype(
        jnp.bfloat16
    )
    for level_idx in range(local_levels):
        partner = flip_last(current, 1 << level_idx % local_bits)
        current = mix_local(local_mats[level_idx], current, partner, phases[level_idx])
    for level_idx in range(cross_levels):
        level_bit = (box_bits - 1 - level_idx) % box_bits
        partner = swapped(current, "box", level_bit)
        current = mix_local(
            cross_mats[level_idx], current, partner, phases[local_levels + level_idx]
        )
    shaped = current.reshape(rank_dim, box_count, group_size)
    pixels_out = jnp.einsum(
        "qr,rdt->qdt",
        evaluate_mats,
        lax.all_to_all(shaped, "box", split_axis=1, concat_axis=1, tiled=True),
        preferred_element_type=jnp.float32,
    )
    return pixels_out.reshape(pixel_rows, local_boxes).astype(jnp.bfloat16)


def xor(a, b, bits):
    out = 0
    for i in range(bits):
        out = out + lax.rem(a // (1 << i) + b // (1 << i), 2) * (1 << i)
    return out


def cos_sin(t):
    u = t * 0.5
    w = u * u
    s = -1.0 / 39916800
    for coef in (1.0 / 362880, -1.0 / 5040, 1.0 / 120, -1.0 / 6, 1.0):
        s = s * w + coef
    s = s * u
    c = 1.0 / 479001600
    for coef in (-1.0 / 3628800, 1.0 / 40320, -1.0 / 720, 1.0 / 24, -0.5, 1.0):
        c = c * w + coef
    return 1.0 - 2.0 * s * s, 2.0 * s * c


def mix(matrix, own, partner, cos, sin):
    stacked = jnp.concatenate([(cos * own).astype(BF16), (sin * partner).astype(BF16)], axis=0)
    return jnp.dot(matrix, stacked, preferred_element_type=F32)


def lane_partner(x, span):
    lo, hi = x[:, :LANES], x[:, LANES:]
    if span == LANES:
        return jnp.concatenate([hi, lo], axis=1)
    index = lax.broadcasted_iota(jnp.int32, lo.shape, 1)
    index = jnp.bitwise_xor(index, span)
    parts = [jnp.take_along_axis(p, index, axis=1, mode="promise_in_bounds") for p in (lo, hi)]
    return jnp.concatenate(parts, axis=1)


def kernel(
    n_box, src_hbm, proj_hbm, local_hbm, cross_hbm, ang_hbm, eval_hbm, out_ref,
    src_ref, proj_ref, local_ref, cross_ref, ang_ref, eval_t_ref, eval_ref,
    snd, rcv, aux, ang_out, local_w, in_sem, src_sem,
    s_snd, s_rcv, w_snd, w_rcv, a_snd, a_rcv, q_snd, q_rcv,
):
    bits = n_box.bit_length() - 1
    n_local, n_cross = local_ref.shape[0], cross_ref.shape[0]
    rank = proj_ref.shape[0]
    n_sub = rank // TILE
    group = src_hbm.shape[1] // n_box
    w_rows = n_cross * TILE
    me = lax.axis_index("box")
    part = lax.axis_index("src")

    def peer(d):
        return xor(me, d, bits)

    def to_box(d):
        return (peer(d), part)

    part_y, part_c = xor(part, 2, 2), xor(part, 1, 2)
    barrier = pltpu.get_barrier_semaphore()
    for target in [to_box(d) for d in range(1, n_box)] + [(me, part_y), (me, part_c)]:
        pl.semaphore_signal(barrier, inc=1, device_id=target, device_id_type=MESH)

    def load(i, source, target):
        return pltpu.make_async_copy(source, target, in_sem.at[i])

    loads = [
        load(i, *pair)
        for i, pair in enumerate([
            (proj_hbm, proj_ref), (ang_hbm, ang_ref), (local_hbm, local_ref),
            (cross_hbm, cross_ref), (eval_hbm, eval_t_ref),
        ])
    ]

    def columns(sub, d):
        return pl.ds(pl.multiple_of(peer(d) * group + sub * UNIT, UNIT), UNIT)

    def load_source(sub, d):
        return pltpu.make_async_copy(
            src_hbm.at[:, columns(sub, d)], src_ref.at[sub, d], src_sem.at[sub, d]
        )

    far = n_box // 2
    order = list(range(far, n_box)) + list(range(far - 1, -1, -1))

    def start_unit(sub):
        for d in order:
            load_source(sub, d).start()

    for copy in loads[:3]:
        copy.start()
    start_unit(0)
    for copy in loads[3:]:
        copy.start()

    def start_rest(it, carry):
        start_unit(it)
        return carry

    lax.fori_loop(1, n_sub, start_rest, 0)
    for copy in loads[:3]:
        copy.wait()
    for l in range(n_local):
        local_w[l] = jnp.concatenate([local_ref[l, 0], local_ref[l, 1]], axis=1)

    def angle_tile(d):
        block = ang_ref[:, columns(part, d)].astype(F32)[n_local:n_local + n_cross]
        block = jnp.concatenate([block, jnp.zeros((8 - n_cross, UNIT), F32)], axis=0)
        return jnp.concatenate([block[:, :LANES], block[:, LANES:]], axis=0).astype(BF16)

    def prepare_aux():
        for copy in loads[3:]:
            copy.wait()
        for m in range(n_cross):
            rows = pl.ds(pl.multiple_of(part * TILE, TILE), TILE)
            aux[part, me, m * TILE:(m + 1) * TILE, :] = jnp.concatenate(
                [cross_ref[m, 0, rows, :], cross_ref[m, 1, rows, :]], axis=1
            )
        aux[part, me, w_rows:w_rows + TILE, :] = angle_tile(0)
        for d in range(1, n_box):
            ang_out[d] = angle_tile(d)

    def w_copy(d):
        low = d if d <= far else d - far
        piece = aux.at[part, peer(d - low), 0:w_rows]
        return pltpu.make_async_remote_copy(
            src_ref=piece, dst_ref=piece, send_sem=w_snd.at[d], recv_sem=w_rcv.at[d],
            device_id=to_box(low), device_id_type=MESH,
        )

    def a_copy(d):
        return pltpu.make_async_remote_copy(
            src_ref=ang_out.at[d], dst_ref=aux.at[part, me, w_rows:w_rows + TILE],
            send_sem=a_snd.at[d], recv_sem=a_rcv.at[d],
            device_id=to_box(d), device_id_type=MESH,
        )

    def q_copy(i):
        quarter = part if i < 2 else part_y
        return pltpu.make_async_remote_copy(
            src_ref=aux.at[quarter], dst_ref=aux.at[quarter],
            send_sem=q_snd.at[i], recv_sem=q_rcv.at[i],
            device_id=(me, part_y if i == 0 else part_c), device_id_type=MESH,
        )

    def s_copy(sub, d):
        return pltpu.make_async_remote_copy(
            src_ref=snd.at[sub, d], dst_ref=rcv.at[sub, me],
            send_sem=s_snd.at[sub, d], recv_sem=s_rcv.at[sub, d],
            device_id=to_box(d), device_id_type=MESH,
        )

    def local_levels(sub, chosen, midway):
        xs, cs, ss = {}, {}, {}
        for d in chosen:
            load_source(sub, d).wait()
        for d in chosen:
            xs[d] = jnp.dot(proj_ref[...], src_ref[sub, d], preferred_element_type=F32)
            cs[d], ss[d] = cos_sin(ang_ref[:, columns(sub, d)].astype(F32)[:n_local])
        for l in range(n_local):
            if l == n_local // 2:
                midway()
            matrix = local_w[l]
            for d in chosen:
                x = xs[d]
                xs[d] = mix(matrix, x, lane_partner(x, 1 << l), cs[d][l:l + 1], ss[d][l:l + 1])
        for d in chosen:
            if d:
                snd[sub, d] = xs[d].astype(BF16)
                s_copy(sub, d).start()
            else:
                rcv[sub, me] = xs[0].astype(BF16)

    def send_aux():
        pl.semaphore_wait(barrier, n_box + 1)
        prepare_aux()
        for d in range(far, 0, -1):
            w_copy(d).start()
        for d in range(n_box - 1, 0, -1):
            a_copy(d).start()

    def forward_aux():
        w_copy(far).wait_recv()
        for d in range(far + 1, n_box):
            w_copy(d).start()

    local_levels(0, order[:far], send_aux)
    local_levels(0, order[far:], forward_aux)

    def local_step(sub, carry):
        def share_aux():
            @pl.when(sub == 1)
            def _():
                for d in range(1, n_box):
                    if d != far:
                        w_copy(d).wait_recv()
                    a_copy(d).wait_recv()
                q_copy(0).start()
                q_copy(1).start()

            @pl.when(sub == n_sub - 1)
            def _():
                q_copy(0).wait_recv()
                q_copy(2).start()

        local_levels(sub, order, share_aux)
        return carry

    lax.fori_loop(1, n_sub, local_step, 0)
    eval_ref[...] = eval_t_ref[...].astype(F32).T.astype(BF16)
    q_copy(1).wait_recv()
    q_copy(2).wait_recv()

    def cross_step(sub, carry):
        for d in range(1, n_box):
            s_copy(sub, d).wait_recv()
        xs = [rcv[sub, k].astype(F32) for k in range(n_box)]
        tables = [cos_sin(aux[sub, k, w_rows:w_rows + TILE, :].astype(F32)) for k in range(n_box)]

        def row(table, m):
            return jnp.concatenate([table[m:m + 1], table[8 + m:9 + m]], axis=1)

        for m in range(n_cross):
            bit = 1 << (bits - 1 - m) % bits
            new = []
            for k in range(n_box):
                matrix = jnp.concatenate(
                    [aux[q, k, m * TILE:(m + 1) * TILE, :] for q in range(n_sub)], axis=0
                )
                cos, sin = tables[k]
                new.append(mix(matrix, xs[k], xs[k ^ bit], row(cos, m), row(sin, m)))
            xs = new
        for k in range(n_box):
            pixels = jnp.dot(eval_ref[...], xs[k].astype(BF16), preferred_element_type=F32)
            start = pl.multiple_of(k * group + sub * UNIT, UNIT)
            out_ref[:, pl.ds(start, UNIT)] = pixels.astype(BF16)
        return carry

    lax.fori_loop(0, n_sub, cross_step, 0)

    def drain(sub, carry):
        for d in range(1, n_box):
            s_copy(sub, d).wait_send()
        return carry

    lax.fori_loop(0, n_sub, drain, 0)
    for d in range(1, n_box):
        w_copy(d).wait_send()
        a_copy(d).wait_send()
    for i in range(3):
        q_copy(i).wait_send()


def shards(source_field, project_mats, local_mats, cross_mats, angles, evaluate_mats):
    n_box = lax.axis_size("box")
    rank = project_mats.shape[0]
    n_sub = rank // TILE
    n_cross = cross_mats.shape[0]
    boxes = source_field.shape[1]
    pixels = evaluate_mats.shape[0]
    rows = n_cross * TILE + TILE
    dma = pltpu.SemaphoreType.DMA
    flops = 2 * boxes * rank * (2 * pixels + 2 * rank * angles.shape[0])
    return pl.pallas_call(
        functools.partial(kernel, n_box),
        out_shape=pltpu.VMEM((pixels, boxes), BF16),
        in_specs=[pl.BlockSpec(memory_space=pltpu.HBM)] * 6,
        out_specs=pl.BlockSpec(memory_space=pltpu.VMEM),
        scratch_shapes=[
            pltpu.VMEM((n_sub, n_box, pixels, UNIT), BF16),
            pltpu.VMEM(project_mats.shape, BF16),
            pltpu.VMEM(local_mats.shape, BF16),
            pltpu.VMEM(cross_mats.shape, BF16),
            pltpu.VMEM(angles.shape, BF16),
            pltpu.VMEM((rank, pixels), BF16),
            pltpu.VMEM((pixels, rank), BF16),
            pltpu.VMEM((n_sub, n_box, rank, UNIT), BF16),
            pltpu.VMEM((n_sub, n_box, rank, UNIT), BF16),
            pltpu.VMEM((n_sub, n_box, rows, LANES), BF16),
            pltpu.VMEM((n_box, TILE, LANES), BF16),
            pltpu.VMEM((local_mats.shape[0], rank, 2 * rank), BF16),
            dma((5,)), dma((n_sub, n_box)),
            dma((n_sub, n_box)), dma((n_sub, n_box)),
            dma((n_box,)), dma((n_box,)),
            dma((n_box,)), dma((n_box,)),
            dma((3,)), dma((3,)),
        ],
        compiler_params=pltpu.CompilerParams(
            collective_id=0, has_side_effects=True, vmem_limit_bytes=60 * 1024 * 1024
        ),
        cost_estimate=pl.CostEstimate(
            flops=flops, bytes_accessed=4 * boxes * pixels, transcendentals=0
        ),
    )(source_field, project_mats, local_mats, cross_mats, angles, evaluate_mats.T)


def fits_kernel(mesh):
    return mesh.shape["box"] == 8 and mesh.shape["src"] == 4


def solution(mesh):
    in_specs = (
        P("src", "box"),
        P("box", None),
        P(None, None, "box", None),
        P(None, None, "box", None),
        P(None, "box"),
        P("box", None),
    )
    out_specs = P("src", "box")
    body = shards if fits_kernel(mesh) else plain_shards
    return jax.shard_map(body, mesh=mesh, in_specs=in_specs, out_specs=out_specs, check_vma=False)
```

```python
import functools

import jax
import jax.numpy as jnp
from jax import lax
from jax.experimental import pallas as pl
from jax.experimental.pallas import tpu as pltpu
from jax.sharding import PartitionSpec as P

MESH = pl.DeviceIdType.MESH
F32 = jnp.float32
BF16 = jnp.bfloat16
LANES = 128
TILE = 16
UNIT = 256


def swapped(x, axis, distance):
    return lax.ppermute(x, axis, [(i, i ^ 1 << distance) for i in range(lax.axis_size(axis))])


def flip_last(values, pair_span):
    full_shape = values.shape
    leading = full_shape[:-1]
    reshaped = values.reshape(leading + (full_shape[-1] // (2 * pair_span), 2, pair_span))
    return jnp.flip(reshaped, axis=-2).reshape(full_shape)


def mix_local(matrices, current, partner, phase_row):
    own_term = jnp.dot(matrices[0], current, preferred_element_type=jnp.float32)
    partner_term = jnp.dot(matrices[1], partner, preferred_element_type=jnp.float32)
    return (jnp.cos(phase_row)[None] * own_term + jnp.sin(phase_row)[None] * partner_term).astype(
        jnp.bfloat16
    )


def plain_shards(source_field, project_mats, local_mats, cross_mats, angles, evaluate_mats):
    box_count = lax.axis_size("box")
    local_boxes = source_field.shape[1]
    rank_dim = project_mats.shape[0]
    pixel_rows = evaluate_mats.shape[0]
    local_levels = local_mats.shape[0]
    cross_levels = cross_mats.shape[0]
    group_size = local_boxes // box_count
    local_bits = (local_boxes & -local_boxes).bit_length() - 1
    box_bits = box_count.bit_length() - 1
    phases = angles.astype(jnp.float32)
    current = jnp.dot(project_mats, source_field, preferred_element_type=jnp.float32).astype(
        jnp.bfloat16
    )
    for level_idx in range(local_levels):
        partner = flip_last(current, 1 << level_idx % local_bits)
        current = mix_local(local_mats[level_idx], current, partner, phases[level_idx])
    for level_idx in range(cross_levels):
        level_bit = (box_bits - 1 - level_idx) % box_bits
        partner = swapped(current, "box", level_bit)
        current = mix_local(
            cross_mats[level_idx], current, partner, phases[local_levels + level_idx]
        )
    shaped = current.reshape(rank_dim, box_count, group_size)
    pixels_out = jnp.einsum(
        "qr,rdt->qdt",
        evaluate_mats,
        lax.all_to_all(shaped, "box", split_axis=1, concat_axis=1, tiled=True),
        preferred_element_type=jnp.float32,
    )
    return pixels_out.reshape(pixel_rows, local_boxes).astype(jnp.bfloat16)


def xor(a, b, bits):
    out = 0
    for i in range(bits):
        out = out + lax.rem(a // (1 << i) + b // (1 << i), 2) * (1 << i)
    return out


def cos_sin(t):
    u = t * 0.5
    w = u * u
    s = -1.0 / 39916800
    for coef in (1.0 / 362880, -1.0 / 5040, 1.0 / 120, -1.0 / 6, 1.0):
        s = s * w + coef
    s = s * u
    c = 1.0 / 479001600
    for coef in (-1.0 / 3628800, 1.0 / 40320, -1.0 / 720, 1.0 / 24, -0.5, 1.0):
        c = c * w + coef
    return 1.0 - 2.0 * s * s, 2.0 * s * c


def mix(matrix, own, partner, cos, sin):
    stacked = jnp.concatenate([(cos * own).astype(BF16), (sin * partner).astype(BF16)], axis=0)
    return jnp.dot(matrix, stacked, preferred_element_type=F32)


def lane_partner(x, span):
    lo, hi = x[:, :LANES], x[:, LANES:]
    if span == LANES:
        return jnp.concatenate([hi, lo], axis=1)
    index = lax.broadcasted_iota(jnp.int32, lo.shape, 1)
    index = jnp.bitwise_xor(index, span)
    parts = [jnp.take_along_axis(p, index, axis=1, mode="promise_in_bounds") for p in (lo, hi)]
    return jnp.concatenate(parts, axis=1)


def kernel(
    n_box, src_hbm, proj_hbm, local_hbm, cross_hbm, ang_hbm, eval_hbm, out_ref,
    src_ref, proj_ref, local_ref, cross_ref, ang_ref, eval_t_ref, eval_ref,
    snd, rcv, aux, ang_out, local_w, in_sem, src_sem,
    s_snd, s_rcv, w_snd, w_rcv, a_snd, a_rcv, q_snd, q_rcv,
):
    bits = n_box.bit_length() - 1
    n_local, n_cross = local_ref.shape[0], cross_ref.shape[0]
    rank = proj_ref.shape[0]
    n_sub = rank // TILE
    group = src_hbm.shape[1] // n_box
    w_rows = n_cross * TILE
    me = lax.axis_index("box")
    part = lax.axis_index("src")

    def peer(d):
        return xor(me, d, bits)

    def to_box(d):
        return (peer(d), part)

    part_y, part_c = xor(part, 2, 2), xor(part, 1, 2)
    barrier = pltpu.get_barrier_semaphore()
    for target in [to_box(d) for d in range(1, n_box)] + [(me, part_y), (me, part_c)]:
        pl.semaphore_signal(barrier, inc=1, device_id=target, device_id_type=MESH)

    def load(i, source, target):
        return pltpu.make_async_copy(source, target, in_sem.at[i])

    loads = [
        load(i, *pair)
        for i, pair in enumerate([
            (proj_hbm, proj_ref), (ang_hbm, ang_ref), (local_hbm, local_ref),
            (cross_hbm, cross_ref), (eval_hbm, eval_t_ref),
        ])
    ]

    def columns(sub, d):
        return pl.ds(pl.multiple_of(peer(d) * group + sub * UNIT, UNIT), UNIT)

    def load_source(sub, d):
        return pltpu.make_async_copy(
            src_hbm.at[:, columns(sub, d)], src_ref.at[sub, d], src_sem.at[sub, d]
        )

    far = n_box // 2
    order = list(range(far, n_box)) + list(range(far - 1, -1, -1))

    def start_unit(sub):
        for d in order:
            load_source(sub, d).start()

    for copy in loads[:3]:
        copy.start()
    start_unit(0)
    for copy in loads[3:]:
        copy.start()

    def start_rest(it, carry):
        start_unit(it)
        return carry

    lax.fori_loop(1, n_sub, start_rest, 0)
    for copy in loads[:3]:
        copy.wait()
    for l in range(n_local):
        local_w[l] = jnp.concatenate([local_ref[l, 0], local_ref[l, 1]], axis=1)

    def angle_tile(d):
        block = ang_ref[:, columns(part, d)].astype(F32)[n_local:n_local + n_cross]
        block = jnp.concatenate([block, jnp.zeros((8 - n_cross, UNIT), F32)], axis=0)
        return jnp.concatenate([block[:, :LANES], block[:, LANES:]], axis=0).astype(BF16)

    def prepare_aux():
        for copy in loads[3:]:
            copy.wait()
        for m in range(n_cross):
            rows = pl.ds(pl.multiple_of(part * TILE, TILE), TILE)
            aux[part, me, m * TILE:(m + 1) * TILE, :] = jnp.concatenate(
                [cross_ref[m, 0, rows, :], cross_ref[m, 1, rows, :]], axis=1
            )
        aux[part, me, w_rows:w_rows + TILE, :] = angle_tile(0)
        for d in range(1, n_box):
            ang_out[d] = angle_tile(d)

    def w_copy(d):
        low = d if d <= far else d - far
        piece = aux.at[part, peer(d - low), 0:w_rows]
        return pltpu.make_async_remote_copy(
            src_ref=piece, dst_ref=piece, send_sem=w_snd.at[d], recv_sem=w_rcv.at[d],
            device_id=to_box(low), device_id_type=MESH,
        )

    def a_copy(d):
        return pltpu.make_async_remote_copy(
            src_ref=ang_out.at[d], dst_ref=aux.at[part, me, w_rows:w_rows + TILE],
            send_sem=a_snd.at[d], recv_sem=a_rcv.at[d],
            device_id=to_box(d), device_id_type=MESH,
        )

    def q_copy(i):
        quarter = part if i < 2 else part_y
        return pltpu.make_async_remote_copy(
            src_ref=aux.at[quarter], dst_ref=aux.at[quarter],
            send_sem=q_snd.at[i], recv_sem=q_rcv.at[i],
            device_id=(me, part_y if i == 0 else part_c), device_id_type=MESH,
        )

    def s_copy(sub, d, half=None):
        lanes = pl.ds(0, UNIT) if half is None else pl.ds(half * LANES, LANES)
        slot = sub if half is None else sub + half
        return pltpu.make_async_remote_copy(
            src_ref=snd.at[sub, d, :, lanes], dst_ref=rcv.at[sub, me, :, lanes],
            send_sem=s_snd.at[slot, d], recv_sem=s_rcv.at[slot, d],
            device_id=to_box(d), device_id_type=MESH,
        )

    last = n_sub - 1

    def local_levels(sub, chosen, midway):
        xs, cs, ss = {}, {}, {}
        for d in chosen:
            load_source(sub, d).wait()
        for d in chosen:
            xs[d] = jnp.dot(proj_ref[...], src_ref[sub, d], preferred_element_type=F32)
            cs[d], ss[d] = cos_sin(ang_ref[:, columns(sub, d)].astype(F32)[:n_local])
        for l in range(n_local):
            if l == n_local // 2:
                midway()
            matrix = local_w[l]
            for d in chosen:
                x = xs[d]
                xs[d] = mix(matrix, x, lane_partner(x, 1 << l), cs[d][l:l + 1], ss[d][l:l + 1])
        for d in chosen:
            if d:
                snd[sub, d] = xs[d].astype(BF16)
            else:
                rcv[sub, me] = xs[0].astype(BF16)
        away = [d for d in chosen if d]

        @pl.when(sub < last)
        def _():
            for d in away:
                s_copy(sub, d).start()

        @pl.when(sub == last)
        def _():
            for half in range(2):
                for d in away:
                    s_copy(last, d, half).start()

    def send_aux():
        pl.semaphore_wait(barrier, n_box + 1)
        prepare_aux()
        for d in range(far, 0, -1):
            w_copy(d).start()
        for d in range(n_box - 1, 0, -1):
            a_copy(d).start()

    def forward_aux():
        w_copy(far).wait_recv()
        for d in range(far + 1, n_box):
            w_copy(d).start()

    local_levels(0, order[:far], send_aux)
    local_levels(0, order[far:], forward_aux)

    def local_step(sub, carry):
        def share_aux():
            @pl.when(sub == 1)
            def _():
                for d in range(1, n_box):
                    if d != far:
                        w_copy(d).wait_recv()
                    a_copy(d).wait_recv()
                q_copy(0).start()
                q_copy(1).start()

            @pl.when(sub == n_sub - 1)
            def _():
                q_copy(0).wait_recv()
                q_copy(2).start()

        local_levels(sub, order, share_aux)
        return carry

    lax.fori_loop(1, n_sub, local_step, 0)
    eval_ref[...] = eval_t_ref[...].astype(F32).T.astype(BF16)
    q_copy(1).wait_recv()
    q_copy(2).wait_recv()

    def cross_levels(sub, halves):
        width = LANES * len(halves)
        lanes = pl.ds(halves[0] * LANES, width)
        xs = [rcv[sub, k, :, lanes] for k in range(n_box)]
        tables = [cos_sin(aux[sub, k, w_rows:w_rows + TILE, :].astype(F32)) for k in range(n_box)]

        def rows(table, m):
            row = jnp.concatenate([table[8 * h + m:8 * h + m + 1] for h in halves], axis=1)
            return jnp.broadcast_to(row, (TILE, width)).astype(BF16)

        def scale(factor, x):
            return (x.reshape(rank // TILE, TILE, width) * factor[None]).reshape(rank, width)

        for m in range(n_cross):
            bit = 1 << (bits - 1 - m) % bits
            new = []
            for k in range(n_box):
                matrix = jnp.concatenate(
                    [aux[q, k, m * TILE:(m + 1) * TILE, :] for q in range(n_sub)], axis=0
                )
                cos, sin = tables[k]
                stacked = jnp.concatenate(
                    [scale(rows(cos, m), xs[k]), scale(rows(sin, m), xs[k ^ bit])], axis=0
                )
                new.append(jnp.dot(matrix, stacked, preferred_element_type=F32).astype(BF16))
            xs = new
        for k in range(n_box):
            pixels = jnp.dot(eval_ref[...], xs[k], preferred_element_type=F32)
            start = pl.multiple_of(k * group + sub * UNIT + halves[0] * LANES, LANES)
            out_ref[:, pl.ds(start, width)] = pixels.astype(BF16)

    def cross_step(sub, carry):
        for d in range(1, n_box):
            s_copy(sub, d).wait_recv()
        cross_levels(sub, (0, 1))
        return carry

    lax.fori_loop(0, last, cross_step, 0)
    for half in range(2):
        for d in range(1, n_box):
            s_copy(last, d, half).wait_recv()
        cross_levels(last, (half,))

    def drain(sub, carry):
        for d in range(1, n_box):
            s_copy(sub, d).wait_send()
        return carry

    lax.fori_loop(0, last, drain, 0)
    for half in range(2):
        for d in range(1, n_box):
            s_copy(last, d, half).wait_send()
    for d in range(1, n_box):
        w_copy(d).wait_send()
        a_copy(d).wait_send()
    for i in range(3):
        q_copy(i).wait_send()


def shards(source_field, project_mats, local_mats, cross_mats, angles, evaluate_mats):
    n_box = lax.axis_size("box")
    rank = project_mats.shape[0]
    n_sub = rank // TILE
    n_cross = cross_mats.shape[0]
    boxes = source_field.shape[1]
    pixels = evaluate_mats.shape[0]
    rows = n_cross * TILE + TILE
    dma = pltpu.SemaphoreType.DMA
    flops = 2 * boxes * rank * (2 * pixels + 2 * rank * angles.shape[0])
    return pl.pallas_call(
        functools.partial(kernel, n_box),
        out_shape=pltpu.VMEM((pixels, boxes), BF16),
        in_specs=[pl.BlockSpec(memory_space=pltpu.HBM)] * 6,
        out_specs=pl.BlockSpec(memory_space=pltpu.VMEM),
        scratch_shapes=[
            pltpu.VMEM((n_sub, n_box, pixels, UNIT), BF16),
            pltpu.VMEM(project_mats.shape, BF16),
            pltpu.VMEM(local_mats.shape, BF16),
            pltpu.VMEM(cross_mats.shape, BF16),
            pltpu.VMEM(angles.shape, BF16),
            pltpu.VMEM((rank, pixels), BF16),
            pltpu.VMEM((pixels, rank), BF16),
            pltpu.VMEM((n_sub, n_box, rank, UNIT), BF16),
            pltpu.VMEM((n_sub, n_box, rank, UNIT), BF16),
            pltpu.VMEM((n_sub, n_box, rows, LANES), BF16),
            pltpu.VMEM((n_box, TILE, LANES), BF16),
            pltpu.VMEM((local_mats.shape[0], rank, 2 * rank), BF16),
            dma((5,)), dma((n_sub, n_box)),
            dma((n_sub + 1, n_box)), dma((n_sub + 1, n_box)),
            dma((n_box,)), dma((n_box,)),
            dma((n_box,)), dma((n_box,)),
            dma((3,)), dma((3,)),
        ],
        compiler_params=pltpu.CompilerParams(
            collective_id=0, has_side_effects=True, vmem_limit_bytes=60 * 1024 * 1024
        ),
        cost_estimate=pl.CostEstimate(
            flops=flops, bytes_accessed=4 * boxes * pixels, transcendentals=0
        ),
    )(source_field, project_mats, local_mats, cross_mats, angles, evaluate_mats.T)


def fits_kernel(mesh):
    return mesh.shape["box"] == 8 and mesh.shape["src"] == 4


def solution(mesh):
    in_specs = (
        P("src", "box"),
        P("box", None),
        P(None, None, "box", None),
        P(None, None, "box", None),
        P(None, "box"),
        P("box", None),
    )
    out_specs = P("src", "box")
    body = shards if fits_kernel(mesh) else plain_shards
    return jax.shard_map(body, mesh=mesh, in_specs=in_specs, out_specs=out_specs, check_vma=False)
```

```python
import functools

import jax
import jax.numpy as jnp
from jax import lax
from jax.experimental import pallas as pl
from jax.experimental.pallas import tpu as pltpu
from jax.sharding import PartitionSpec as P

MESH = pl.DeviceIdType.MESH
F32 = jnp.float32
BF16 = jnp.bfloat16
LANES = 128
TILE = 16
UNIT = 256


def swapped(x, axis, distance):
    return lax.ppermute(x, axis, [(i, i ^ 1 << distance) for i in range(lax.axis_size(axis))])


def flip_last(values, pair_span):
    full_shape = values.shape
    leading = full_shape[:-1]
    reshaped = values.reshape(leading + (full_shape[-1] // (2 * pair_span), 2, pair_span))
    return jnp.flip(reshaped, axis=-2).reshape(full_shape)


def mix_local(matrices, current, partner, phase_row):
    own_term = jnp.dot(matrices[0], current, preferred_element_type=jnp.float32)
    partner_term = jnp.dot(matrices[1], partner, preferred_element_type=jnp.float32)
    return (jnp.cos(phase_row)[None] * own_term + jnp.sin(phase_row)[None] * partner_term).astype(
        jnp.bfloat16
    )


def plain_shards(source_field, project_mats, local_mats, cross_mats, angles, evaluate_mats):
    box_count = lax.axis_size("box")
    local_boxes = source_field.shape[1]
    rank_dim = project_mats.shape[0]
    pixel_rows = evaluate_mats.shape[0]
    local_levels = local_mats.shape[0]
    cross_levels = cross_mats.shape[0]
    group_size = local_boxes // box_count
    local_bits = (local_boxes & -local_boxes).bit_length() - 1
    box_bits = box_count.bit_length() - 1
    phases = angles.astype(jnp.float32)
    current = jnp.dot(project_mats, source_field, preferred_element_type=jnp.float32).astype(
        jnp.bfloat16
    )
    for level_idx in range(local_levels):
        partner = flip_last(current, 1 << level_idx % local_bits)
        current = mix_local(local_mats[level_idx], current, partner, phases[level_idx])
    for level_idx in range(cross_levels):
        level_bit = (box_bits - 1 - level_idx) % box_bits
        partner = swapped(current, "box", level_bit)
        current = mix_local(
            cross_mats[level_idx], current, partner, phases[local_levels + level_idx]
        )
    shaped = current.reshape(rank_dim, box_count, group_size)
    pixels_out = jnp.einsum(
        "qr,rdt->qdt",
        evaluate_mats,
        lax.all_to_all(shaped, "box", split_axis=1, concat_axis=1, tiled=True),
        preferred_element_type=jnp.float32,
    )
    return pixels_out.reshape(pixel_rows, local_boxes).astype(jnp.bfloat16)


def xor(a, b, bits):
    out = 0
    for i in range(bits):
        out = out + lax.rem(a // (1 << i) + b // (1 << i), 2) * (1 << i)
    return out


def cos_sin(t):
    u = t * 0.5
    w = u * u
    s = -1.0 / 39916800
    for coef in (1.0 / 362880, -1.0 / 5040, 1.0 / 120, -1.0 / 6, 1.0):
        s = s * w + coef
    s = s * u
    c = 1.0 / 479001600
    for coef in (-1.0 / 3628800, 1.0 / 40320, -1.0 / 720, 1.0 / 24, -0.5, 1.0):
        c = c * w + coef
    return 1.0 - 2.0 * s * s, 2.0 * s * c


def mix(matrix, own, partner, cos, sin):
    stacked = jnp.concatenate([(cos * own).astype(BF16), (sin * partner).astype(BF16)], axis=0)
    return jnp.dot(matrix, stacked, preferred_element_type=F32)


def lane_partner(x, span):
    lo, hi = x[:, :LANES], x[:, LANES:]
    if span == LANES:
        return jnp.concatenate([hi, lo], axis=1)
    index = lax.broadcasted_iota(jnp.int32, lo.shape, 1)
    index = jnp.bitwise_xor(index, span)
    parts = [jnp.take_along_axis(p, index, axis=1, mode="promise_in_bounds") for p in (lo, hi)]
    return jnp.concatenate(parts, axis=1)


def kernel(
    n_box, src_hbm, proj_hbm, local_hbm, cross_hbm, ang_hbm, eval_hbm, out_ref,
    src_ref, proj_ref, local_ref, cross_ref, ang_ref, eval_t_ref, eval_ref,
    snd, rcv, aux, ang_out, local_w, in_sem, src_sem,
    s_snd, s_rcv, w_snd, w_rcv, a_snd, a_rcv, q_snd, q_rcv,
):
    bits = n_box.bit_length() - 1
    n_local, n_cross = local_ref.shape[0], cross_ref.shape[0]
    rank = proj_ref.shape[0]
    n_sub = rank // TILE
    group = src_hbm.shape[1] // n_box
    w_rows = n_cross * TILE
    me = lax.axis_index("box")
    part = lax.axis_index("src")

    def peer(d):
        return xor(me, d, bits)

    def to_box(d):
        return (peer(d), part)

    part_y, part_c = xor(part, 2, 2), xor(part, 1, 2)
    barrier = pltpu.get_barrier_semaphore()
    for target in [to_box(d) for d in range(1, n_box)] + [(me, part_y), (me, part_c)]:
        pl.semaphore_signal(barrier, inc=1, device_id=target, device_id_type=MESH)

    def load(i, source, target):
        return pltpu.make_async_copy(source, target, in_sem.at[i])

    loads = [
        load(i, *pair)
        for i, pair in enumerate([
            (proj_hbm, proj_ref), (ang_hbm, ang_ref), (local_hbm, local_ref),
            (cross_hbm, cross_ref), (eval_hbm, eval_t_ref),
        ])
    ]

    def columns(sub, d):
        return pl.ds(pl.multiple_of(peer(d) * group + sub * UNIT, UNIT), UNIT)

    def load_source(sub, d):
        return pltpu.make_async_copy(
            src_hbm.at[:, columns(sub, d)], src_ref.at[sub, d], src_sem.at[sub, d]
        )

    far = n_box // 2
    order = list(range(far, n_box)) + list(range(far - 1, -1, -1))

    def start_unit(sub):
        for d in order:
            load_source(sub, d).start()

    for copy in loads[:3]:
        copy.start()
    start_unit(0)
    for copy in loads[3:]:
        copy.start()

    def start_rest(it, carry):
        start_unit(it)
        return carry

    lax.fori_loop(1, n_sub, start_rest, 0)
    for copy in loads[:3]:
        copy.wait()
    for l in range(n_local):
        local_w[l] = jnp.concatenate([local_ref[l, 0], local_ref[l, 1]], axis=1)

    def angle_tile(d):
        block = ang_ref[:, columns(part, d)].astype(F32)[n_local:n_local + n_cross]
        block = jnp.concatenate([block, jnp.zeros((8 - n_cross, UNIT), F32)], axis=0)
        return jnp.concatenate([block[:, :LANES], block[:, LANES:]], axis=0).astype(BF16)

    def prepare_aux():
        for copy in loads[3:]:
            copy.wait()
        for m in range(n_cross):
            rows = pl.ds(pl.multiple_of(part * TILE, TILE), TILE)
            aux[part, me, m * TILE:(m + 1) * TILE, :] = jnp.concatenate(
                [cross_ref[m, 0, rows, :], cross_ref[m, 1, rows, :]], axis=1
            )
        aux[part, me, w_rows:w_rows + TILE, :] = angle_tile(0)
        for d in range(1, n_box):
            ang_out[d] = angle_tile(d)

    def w_copy(d):
        low = d if d <= far else d - far
        piece = aux.at[part, peer(d - low), 0:w_rows]
        return pltpu.make_async_remote_copy(
            src_ref=piece, dst_ref=piece, send_sem=w_snd.at[d], recv_sem=w_rcv.at[d],
            device_id=to_box(low), device_id_type=MESH,
        )

    def a_copy(d):
        return pltpu.make_async_remote_copy(
            src_ref=ang_out.at[d], dst_ref=aux.at[part, me, w_rows:w_rows + TILE],
            send_sem=a_snd.at[d], recv_sem=a_rcv.at[d],
            device_id=to_box(d), device_id_type=MESH,
        )

    def q_copy(i):
        quarter = part if i < 2 else part_y
        return pltpu.make_async_remote_copy(
            src_ref=aux.at[quarter], dst_ref=aux.at[quarter],
            send_sem=q_snd.at[i], recv_sem=q_rcv.at[i],
            device_id=(me, part_y if i == 0 else part_c), device_id_type=MESH,
        )

    def s_copy(sub, d):
        return pltpu.make_async_remote_copy(
            src_ref=snd.at[sub, d], dst_ref=rcv.at[sub, me],
            send_sem=s_snd.at[sub, d], recv_sem=s_rcv.at[sub, d],
            device_id=to_box(d), device_id_type=MESH,
        )

    def send(sub, chosen):
        away = [d for d in chosen if d]
        far_ones = [d for d in away if d >= far]
        near_ones = [d for d in away if d < far]
        core = lax.rem(part, 2)

        def start(first, second):
            for i in range(max(len(first), len(second))):
                for d in first[i:i + 1] + second[i:i + 1]:
                    s_copy(sub, d).start()

        @pl.when(core == 0)
        def _():
            start(far_ones, near_ones)

        @pl.when(core == 1)
        def _():
            start(near_ones, far_ones)

    def local_levels(sub, chosen, midway):
        xs, cs, ss = {}, {}, {}
        for d in chosen:
            load_source(sub, d).wait()
        for d in chosen:
            xs[d] = jnp.dot(proj_ref[...], src_ref[sub, d], preferred_element_type=F32)
            cs[d], ss[d] = cos_sin(ang_ref[:, columns(sub, d)].astype(F32)[:n_local])
        for l in range(n_local):
            if l == n_local // 2:
                midway()
            matrix = local_w[l]
            for d in chosen:
                x = xs[d]
                xs[d] = mix(matrix, x, lane_partner(x, 1 << l), cs[d][l:l + 1], ss[d][l:l + 1])
        for d in chosen:
            if d:
                snd[sub, d] = xs[d].astype(BF16)
            else:
                rcv[sub, me] = xs[0].astype(BF16)
        send(sub, chosen)

    def send_aux():
        pl.semaphore_wait(barrier, n_box + 1)
        prepare_aux()
        for d in range(far, 0, -1):
            w_copy(d).start()
        for d in range(n_box - 1, 0, -1):
            a_copy(d).start()

    def forward_aux():
        w_copy(far).wait_recv()
        for d in range(far + 1, n_box):
            w_copy(d).start()

    local_levels(0, order[:far], send_aux)
    local_levels(0, order[far:], forward_aux)

    def local_step(sub, carry):
        def share_aux():
            @pl.when(sub == 1)
            def _():
                for d in range(1, n_box):
                    if d != far:
                        w_copy(d).wait_recv()
                    a_copy(d).wait_recv()
                q_copy(0).start()
                q_copy(1).start()

            @pl.when(sub == n_sub - 1)
            def _():
                q_copy(0).wait_recv()
                q_copy(2).start()

        local_levels(sub, order, share_aux)
        return carry

    lax.fori_loop(1, n_sub, local_step, 0)
    eval_ref[...] = eval_t_ref[...].astype(F32).T.astype(BF16)
    q_copy(1).wait_recv()
    q_copy(2).wait_recv()

    def rows(table, m):
        row = jnp.concatenate([table[m:m + 1], table[8 + m:9 + m]], axis=1)
        return jnp.broadcast_to(row, (TILE, UNIT)).astype(BF16)

    def scale(factor, x):
        return (x.reshape(rank // TILE, TILE, UNIT) * factor[None]).reshape(rank, UNIT)

    def cross_levels(subs):
        for sub in subs:
            for d in range(1, n_box):
                s_copy(sub, d).wait_recv()
        chains = [(sub, k) for sub in subs for k in range(n_box)]
        xs = {c: rcv[c[0], c[1]] for c in chains}
        tables = {
            (sub, k): cos_sin(aux[sub, k, w_rows:w_rows + TILE, :].astype(F32)) for sub, k in chains
        }
        for m in range(n_cross):
            bit = 1 << (bits - 1 - m) % bits
            new = {}
            for k in range(n_box):
                matrix = jnp.concatenate(
                    [aux[q, k, m * TILE:(m + 1) * TILE, :] for q in range(n_sub)], axis=0
                )
                for sub in subs:
                    cos, sin = tables[sub, k]
                    stacked = jnp.concatenate(
                        [
                            scale(rows(cos, m), xs[sub, k]),
                            scale(rows(sin, m), xs[sub, k ^ bit]),
                        ],
                        axis=0,
                    )
                    mixed = jnp.dot(matrix, stacked, preferred_element_type=F32)
                    new[sub, k] = mixed.astype(BF16)
            xs = new
        for sub, k in chains:
            pixels = jnp.dot(eval_ref[...], xs[sub, k], preferred_element_type=F32)
            out_ref[:, k * group + sub * UNIT:k * group + (sub + 1) * UNIT] = pixels.astype(BF16)

    for subs in [(0, 1)] + [(sub,) for sub in range(2, n_sub)]:
        cross_levels(subs)

    def drain(sub, carry):
        for d in range(1, n_box):
            s_copy(sub, d).wait_send()
        return carry

    lax.fori_loop(0, n_sub, drain, 0)
    for d in range(1, n_box):
        w_copy(d).wait_send()
        a_copy(d).wait_send()
    for i in range(3):
        q_copy(i).wait_send()


def shards(source_field, project_mats, local_mats, cross_mats, angles, evaluate_mats):
    n_box = lax.axis_size("box")
    rank = project_mats.shape[0]
    n_sub = rank // TILE
    n_cross = cross_mats.shape[0]
    boxes = source_field.shape[1]
    pixels = evaluate_mats.shape[0]
    rows = n_cross * TILE + TILE
    dma = pltpu.SemaphoreType.DMA
    flops = 2 * boxes * rank * (2 * pixels + 2 * rank * angles.shape[0])
    return pl.pallas_call(
        functools.partial(kernel, n_box),
        out_shape=pltpu.VMEM((pixels, boxes), BF16),
        in_specs=[pl.BlockSpec(memory_space=pltpu.HBM)] * 6,
        out_specs=pl.BlockSpec(memory_space=pltpu.VMEM),
        scratch_shapes=[
            pltpu.VMEM((n_sub, n_box, pixels, UNIT), BF16),
            pltpu.VMEM(project_mats.shape, BF16),
            pltpu.VMEM(local_mats.shape, BF16),
            pltpu.VMEM(cross_mats.shape, BF16),
            pltpu.VMEM(angles.shape, BF16),
            pltpu.VMEM((rank, pixels), BF16),
            pltpu.VMEM((pixels, rank), BF16),
            pltpu.VMEM((n_sub, n_box, rank, UNIT), BF16),
            pltpu.VMEM((n_sub, n_box, rank, UNIT), BF16),
            pltpu.VMEM((n_sub, n_box, rows, LANES), BF16),
            pltpu.VMEM((n_box, TILE, LANES), BF16),
            pltpu.VMEM((local_mats.shape[0], rank, 2 * rank), BF16),
            dma((5,)), dma((n_sub, n_box)),
            dma((n_sub, n_box)), dma((n_sub, n_box)),
            dma((n_box,)), dma((n_box,)),
            dma((n_box,)), dma((n_box,)),
            dma((3,)), dma((3,)),
        ],
        compiler_params=pltpu.CompilerParams(
            collective_id=0, has_side_effects=True, vmem_limit_bytes=60 * 1024 * 1024
        ),
        cost_estimate=pl.CostEstimate(
            flops=flops, bytes_accessed=4 * boxes * pixels, transcendentals=0
        ),
    )(source_field, project_mats, local_mats, cross_mats, angles, evaluate_mats.T)


def fits_kernel(mesh):
    return mesh.shape["box"] == 8 and mesh.shape["src"] == 4


def solution(mesh):
    in_specs = (
        P("src", "box"),
        P("box", None),
        P(None, None, "box", None),
        P(None, None, "box", None),
        P(None, "box"),
        P("box", None),
    )
    out_specs = P("src", "box")
    body = shards if fits_kernel(mesh) else plain_shards
    return jax.shard_map(body, mesh=mesh, in_specs=in_specs, out_specs=out_specs, check_vma=False)
```

```python
import functools

import jax
import jax.numpy as jnp
from jax import lax
from jax.experimental import pallas as pl
from jax.experimental.pallas import tpu as pltpu
from jax.sharding import PartitionSpec as P

MESH = pl.DeviceIdType.MESH
F32 = jnp.float32
BF16 = jnp.bfloat16
LANES = 128
TILE = 16
UNIT = 256


def swapped(x, axis, distance):
    return lax.ppermute(x, axis, [(i, i ^ 1 << distance) for i in range(lax.axis_size(axis))])


def flip_last(values, pair_span):
    full_shape = values.shape
    leading = full_shape[:-1]
    reshaped = values.reshape(leading + (full_shape[-1] // (2 * pair_span), 2, pair_span))
    return jnp.flip(reshaped, axis=-2).reshape(full_shape)


def mix_local(matrices, current, partner, phase_row):
    own_term = jnp.dot(matrices[0], current, preferred_element_type=jnp.float32)
    partner_term = jnp.dot(matrices[1], partner, preferred_element_type=jnp.float32)
    return (jnp.cos(phase_row)[None] * own_term + jnp.sin(phase_row)[None] * partner_term).astype(
        jnp.bfloat16
    )


def plain_shards(source_field, project_mats, local_mats, cross_mats, angles, evaluate_mats):
    box_count = lax.axis_size("box")
    local_boxes = source_field.shape[1]
    rank_dim = project_mats.shape[0]
    pixel_rows = evaluate_mats.shape[0]
    local_levels = local_mats.shape[0]
    cross_levels = cross_mats.shape[0]
    group_size = local_boxes // box_count
    local_bits = (local_boxes & -local_boxes).bit_length() - 1
    box_bits = box_count.bit_length() - 1
    phases = angles.astype(jnp.float32)
    current = jnp.dot(project_mats, source_field, preferred_element_type=jnp.float32).astype(
        jnp.bfloat16
    )
    for level_idx in range(local_levels):
        partner = flip_last(current, 1 << level_idx % local_bits)
        current = mix_local(local_mats[level_idx], current, partner, phases[level_idx])
    for level_idx in range(cross_levels):
        level_bit = (box_bits - 1 - level_idx) % box_bits
        partner = swapped(current, "box", level_bit)
        current = mix_local(
            cross_mats[level_idx], current, partner, phases[local_levels + level_idx]
        )
    shaped = current.reshape(rank_dim, box_count, group_size)
    pixels_out = jnp.einsum(
        "qr,rdt->qdt",
        evaluate_mats,
        lax.all_to_all(shaped, "box", split_axis=1, concat_axis=1, tiled=True),
        preferred_element_type=jnp.float32,
    )
    return pixels_out.reshape(pixel_rows, local_boxes).astype(jnp.bfloat16)


def xor(a, b, bits):
    out = 0
    for i in range(bits):
        out = out + lax.rem(a // (1 << i) + b // (1 << i), 2) * (1 << i)
    return out


def cos_sin(t):
    u = t * 0.5
    w = u * u
    s = -1.0 / 39916800
    for coef in (1.0 / 362880, -1.0 / 5040, 1.0 / 120, -1.0 / 6, 1.0):
        s = s * w + coef
    s = s * u
    c = 1.0 / 479001600
    for coef in (-1.0 / 3628800, 1.0 / 40320, -1.0 / 720, 1.0 / 24, -0.5, 1.0):
        c = c * w + coef
    return 1.0 - 2.0 * s * s, 2.0 * s * c


def mix(matrix, own, partner, cos, sin):
    stacked = jnp.concatenate([(cos * own).astype(BF16), (sin * partner).astype(BF16)], axis=0)
    return jnp.dot(matrix, stacked, preferred_element_type=F32)


def lane_partner(x, span):
    lo, hi = x[:, :LANES], x[:, LANES:]
    if span == LANES:
        return jnp.concatenate([hi, lo], axis=1)
    index = lax.broadcasted_iota(jnp.int32, lo.shape, 1)
    index = jnp.bitwise_xor(index, span)
    parts = [jnp.take_along_axis(p, index, axis=1, mode="promise_in_bounds") for p in (lo, hi)]
    return jnp.concatenate(parts, axis=1)


def kernel(
    n_box, src_hbm, proj_hbm, local_hbm, cross_hbm, ang_hbm, eval_hbm, out_ref,
    src_ref, proj_ref, local_ref, cross_ref, ang_ref, eval_t_ref, eval_ref,
    snd, rcv, aux, ang_out, local_w, in_sem, src_sem,
    s_snd, s_rcv, w_snd, w_rcv, a_snd, a_rcv, q_snd, q_rcv,
):
    bits = n_box.bit_length() - 1
    n_local, n_cross = local_ref.shape[0], cross_ref.shape[0]
    rank = proj_ref.shape[0]
    n_sub = rank // TILE
    group = src_hbm.shape[1] // n_box
    w_rows = n_cross * TILE
    me = lax.axis_index("box")
    part = lax.axis_index("src")

    def peer(d):
        return xor(me, d, bits)

    def to_box(d):
        return (peer(d), part)

    part_y, part_c = xor(part, 2, 2), xor(part, 1, 2)
    barrier = pltpu.get_barrier_semaphore()
    for target in [to_box(d) for d in range(1, n_box)] + [(me, part_y), (me, part_c)]:
        pl.semaphore_signal(barrier, inc=1, device_id=target, device_id_type=MESH)

    def load(i, source, target):
        return pltpu.make_async_copy(source, target, in_sem.at[i])

    loads = [
        load(i, *pair)
        for i, pair in enumerate([
            (proj_hbm, proj_ref), (ang_hbm, ang_ref), (local_hbm, local_ref),
            (cross_hbm, cross_ref), (eval_hbm, eval_t_ref),
        ])
    ]

    def columns(sub, d):
        return pl.ds(pl.multiple_of(peer(d) * group + sub * UNIT, UNIT), UNIT)

    def load_source(sub, d):
        return pltpu.make_async_copy(
            src_hbm.at[:, columns(sub, d)], src_ref.at[sub, d], src_sem.at[sub, d]
        )

    far = n_box // 2
    order = list(range(far, n_box)) + list(range(far - 1, -1, -1))

    def start_unit(sub):
        for d in order:
            load_source(sub, d).start()

    for copy in loads[:3]:
        copy.start()
    start_unit(0)
    for copy in loads[3:]:
        copy.start()

    def start_rest(it, carry):
        start_unit(it)
        return carry

    lax.fori_loop(1, n_sub, start_rest, 0)
    for copy in loads[:3]:
        copy.wait()
    for l in range(n_local):
        local_w[l] = jnp.concatenate([local_ref[l, 0], local_ref[l, 1]], axis=1)

    def angle_tile(d):
        block = ang_ref[:, columns(part, d)].astype(F32)[n_local:n_local + n_cross]
        block = jnp.concatenate([block, jnp.zeros((8 - n_cross, UNIT), F32)], axis=0)
        return jnp.concatenate([block[:, :LANES], block[:, LANES:]], axis=0).astype(BF16)

    def prepare_aux():
        for copy in loads[3:]:
            copy.wait()
        for m in range(n_cross):
            rows = pl.ds(pl.multiple_of(part * TILE, TILE), TILE)
            aux[part, me, m * TILE:(m + 1) * TILE, :] = jnp.concatenate(
                [cross_ref[m, 0, rows, :], cross_ref[m, 1, rows, :]], axis=1
            )
        aux[part, me, w_rows:w_rows + TILE, :] = angle_tile(0)
        for d in range(1, n_box):
            ang_out[d] = angle_tile(d)

    def w_copy(d):
        low = d if d <= far else d - far
        piece = aux.at[part, peer(d - low), 0:w_rows]
        return pltpu.make_async_remote_copy(
            src_ref=piece, dst_ref=piece, send_sem=w_snd.at[d], recv_sem=w_rcv.at[d],
            device_id=to_box(low), device_id_type=MESH,
        )

    def a_copy(d):
        return pltpu.make_async_remote_copy(
            src_ref=ang_out.at[d], dst_ref=aux.at[part, me, w_rows:w_rows + TILE],
            send_sem=a_snd.at[d], recv_sem=a_rcv.at[d],
            device_id=to_box(d), device_id_type=MESH,
        )

    def q_copy(i):
        quarter = part if i < 2 else part_y
        return pltpu.make_async_remote_copy(
            src_ref=aux.at[quarter], dst_ref=aux.at[quarter],
            send_sem=q_snd.at[i], recv_sem=q_rcv.at[i],
            device_id=(me, part_y if i == 0 else part_c), device_id_type=MESH,
        )

    def s_copy(sub, d):
        return pltpu.make_async_remote_copy(
            src_ref=snd.at[sub, d], dst_ref=rcv.at[sub, me],
            send_sem=s_snd.at[sub, d], recv_sem=s_rcv.at[sub, d],
            device_id=to_box(d), device_id_type=MESH,
        )

    def local_levels(chosen, midway):
        xs, cs, ss = {}, {}, {}
        for sub, d in chosen:
            load_source(sub, d).wait()
        for sub, d in chosen:
            xs[d] = jnp.dot(proj_ref[...], src_ref[sub, d], preferred_element_type=F32)
            cs[d], ss[d] = cos_sin(ang_ref[:, columns(sub, d)].astype(F32)[:n_local])
        for l in range(n_local):
            if l == n_local // 2:
                midway()
            matrix = local_w[l]
            for _, d in chosen:
                x = xs[d]
                xs[d] = mix(matrix, x, lane_partner(x, 1 << l), cs[d][l:l + 1], ss[d][l:l + 1])
        for sub, d in chosen:
            if d:
                snd[sub, d] = xs[d].astype(BF16)
                s_copy(sub, d).start()
            else:
                rcv[sub, me] = xs[0].astype(BF16)

    def send_aux():
        pl.semaphore_wait(barrier, n_box + 1)
        prepare_aux()
        for d in range(far, 0, -1):
            w_copy(d).start()
        for d in range(n_box - 1, 0, -1):
            a_copy(d).start()

    def forward_aux():
        w_copy(far).wait_recv()
        for d in range(far + 1, n_box):
            w_copy(d).start()

    def far_units(sub):
        return [(sub, d) for d in order[:far]]

    def near_units(sub):
        return [(sub, d) for d in order[far:]]

    local_levels(far_units(0), send_aux)

    def local_step(sub, carry):
        def move_aux():
            @pl.when(sub == 1)
            def _():
                forward_aux()

            @pl.when(sub == 2)
            def _():
                for d in range(1, n_box):
                    if d != far:
                        w_copy(d).wait_recv()
                    a_copy(d).wait_recv()
                q_copy(0).start()
                q_copy(1).start()

        local_levels(far_units(sub) + near_units(sub - 1), move_aux)
        return carry

    def finish_aux():
        q_copy(0).wait_recv()
        q_copy(2).start()

    lax.fori_loop(1, n_sub, local_step, 0)
    local_levels(near_units(n_sub - 1), finish_aux)
    eval_ref[...] = eval_t_ref[...].astype(F32).T.astype(BF16)
    q_copy(1).wait_recv()
    q_copy(2).wait_recv()

    def cross_step(sub, carry):
        for d in range(1, n_box):
            s_copy(sub, d).wait_recv()
        xs = [rcv[sub, k].astype(F32) for k in range(n_box)]
        tables = [cos_sin(aux[sub, k, w_rows:w_rows + TILE, :].astype(F32)) for k in range(n_box)]

        def row(table, m):
            return jnp.concatenate([table[m:m + 1], table[8 + m:9 + m]], axis=1)

        for m in range(n_cross):
            bit = 1 << (bits - 1 - m) % bits
            new = []
            for k in range(n_box):
                matrix = jnp.concatenate(
                    [aux[q, k, m * TILE:(m + 1) * TILE, :] for q in range(n_sub)], axis=0
                )
                cos, sin = tables[k]
                new.append(mix(matrix, xs[k], xs[k ^ bit], row(cos, m), row(sin, m)))
            xs = new
        for k in range(n_box):
            pixels = jnp.dot(eval_ref[...], xs[k].astype(BF16), preferred_element_type=F32)
            start = pl.multiple_of(k * group + sub * UNIT, UNIT)
            out_ref[:, pl.ds(start, UNIT)] = pixels.astype(BF16)
        return carry

    lax.fori_loop(0, n_sub, cross_step, 0)

    def drain(sub, carry):
        for d in range(1, n_box):
            s_copy(sub, d).wait_send()
        return carry

    lax.fori_loop(0, n_sub, drain, 0)
    for d in range(1, n_box):
        w_copy(d).wait_send()
        a_copy(d).wait_send()
    for i in range(3):
        q_copy(i).wait_send()


def shards(source_field, project_mats, local_mats, cross_mats, angles, evaluate_mats):
    n_box = lax.axis_size("box")
    rank = project_mats.shape[0]
    n_sub = rank // TILE
    n_cross = cross_mats.shape[0]
    boxes = source_field.shape[1]
    pixels = evaluate_mats.shape[0]
    rows = n_cross * TILE + TILE
    dma = pltpu.SemaphoreType.DMA
    flops = 2 * boxes * rank * (2 * pixels + 2 * rank * angles.shape[0])
    return pl.pallas_call(
        functools.partial(kernel, n_box),
        out_shape=pltpu.VMEM((pixels, boxes), BF16),
        in_specs=[pl.BlockSpec(memory_space=pltpu.HBM)] * 6,
        out_specs=pl.BlockSpec(memory_space=pltpu.VMEM),
        scratch_shapes=[
            pltpu.VMEM((n_sub, n_box, pixels, UNIT), BF16),
            pltpu.VMEM(project_mats.shape, BF16),
            pltpu.VMEM(local_mats.shape, BF16),
            pltpu.VMEM(cross_mats.shape, BF16),
            pltpu.VMEM(angles.shape, BF16),
            pltpu.VMEM((rank, pixels), BF16),
            pltpu.VMEM((pixels, rank), BF16),
            pltpu.VMEM((n_sub, n_box, rank, UNIT), BF16),
            pltpu.VMEM((n_sub, n_box, rank, UNIT), BF16),
            pltpu.VMEM((n_sub, n_box, rows, LANES), BF16),
            pltpu.VMEM((n_box, TILE, LANES), BF16),
            pltpu.VMEM((local_mats.shape[0], rank, 2 * rank), BF16),
            dma((5,)), dma((n_sub, n_box)),
            dma((n_sub, n_box)), dma((n_sub, n_box)),
            dma((n_box,)), dma((n_box,)),
            dma((n_box,)), dma((n_box,)),
            dma((3,)), dma((3,)),
        ],
        compiler_params=pltpu.CompilerParams(
            collective_id=0, has_side_effects=True, vmem_limit_bytes=60 * 1024 * 1024
        ),
        cost_estimate=pl.CostEstimate(
            flops=flops, bytes_accessed=4 * boxes * pixels, transcendentals=0
        ),
    )(source_field, project_mats, local_mats, cross_mats, angles, evaluate_mats.T)


def fits_kernel(mesh):
    return mesh.shape["box"] == 8 and mesh.shape["src"] == 4


def solution(mesh):
    in_specs = (
        P("src", "box"),
        P("box", None),
        P(None, None, "box", None),
        P(None, None, "box", None),
        P(None, "box"),
        P("box", None),
    )
    out_specs = P("src", "box")
    body = shards if fits_kernel(mesh) else plain_shards
    return jax.shard_map(body, mesh=mesh, in_specs=in_specs, out_specs=out_specs, check_vma=False)
```

```python
import functools

import jax
import jax.numpy as jnp
from jax import lax
from jax.experimental import pallas as pl
from jax.experimental.pallas import tpu as pltpu
from jax.sharding import PartitionSpec as P

MESH = pl.DeviceIdType.MESH
F32 = jnp.float32
BF16 = jnp.bfloat16
LANES = 128
TILE = 16
UNIT = 256


def swapped(x, axis, distance):
    return lax.ppermute(x, axis, [(i, i ^ 1 << distance) for i in range(lax.axis_size(axis))])


def flip_last(values, pair_span):
    full_shape = values.shape
    leading = full_shape[:-1]
    reshaped = values.reshape(leading + (full_shape[-1] // (2 * pair_span), 2, pair_span))
    return jnp.flip(reshaped, axis=-2).reshape(full_shape)


def mix_local(matrices, current, partner, phase_row):
    own_term = jnp.dot(matrices[0], current, preferred_element_type=jnp.float32)
    partner_term = jnp.dot(matrices[1], partner, preferred_element_type=jnp.float32)
    return (jnp.cos(phase_row)[None] * own_term + jnp.sin(phase_row)[None] * partner_term).astype(
        jnp.bfloat16
    )


def plain_shards(source_field, project_mats, local_mats, cross_mats, angles, evaluate_mats):
    box_count = lax.axis_size("box")
    local_boxes = source_field.shape[1]
    rank_dim = project_mats.shape[0]
    pixel_rows = evaluate_mats.shape[0]
    local_levels = local_mats.shape[0]
    cross_levels = cross_mats.shape[0]
    group_size = local_boxes // box_count
    local_bits = (local_boxes & -local_boxes).bit_length() - 1
    box_bits = box_count.bit_length() - 1
    phases = angles.astype(jnp.float32)
    current = jnp.dot(project_mats, source_field, preferred_element_type=jnp.float32).astype(
        jnp.bfloat16
    )
    for level_idx in range(local_levels):
        partner = flip_last(current, 1 << level_idx % local_bits)
        current = mix_local(local_mats[level_idx], current, partner, phases[level_idx])
    for level_idx in range(cross_levels):
        level_bit = (box_bits - 1 - level_idx) % box_bits
        partner = swapped(current, "box", level_bit)
        current = mix_local(
            cross_mats[level_idx], current, partner, phases[local_levels + level_idx]
        )
    shaped = current.reshape(rank_dim, box_count, group_size)
    pixels_out = jnp.einsum(
        "qr,rdt->qdt",
        evaluate_mats,
        lax.all_to_all(shaped, "box", split_axis=1, concat_axis=1, tiled=True),
        preferred_element_type=jnp.float32,
    )
    return pixels_out.reshape(pixel_rows, local_boxes).astype(jnp.bfloat16)


def xor(a, b, bits):
    out = 0
    for i in range(bits):
        out = out + lax.rem(a // (1 << i) + b // (1 << i), 2) * (1 << i)
    return out


def cos_sin(t):
    u = t * 0.5
    w = u * u
    s = -1.0 / 39916800
    for coef in (1.0 / 362880, -1.0 / 5040, 1.0 / 120, -1.0 / 6, 1.0):
        s = s * w + coef
    s = s * u
    c = 1.0 / 479001600
    for coef in (-1.0 / 3628800, 1.0 / 40320, -1.0 / 720, 1.0 / 24, -0.5, 1.0):
        c = c * w + coef
    return 1.0 - 2.0 * s * s, 2.0 * s * c


def mix(matrix, own, partner, cos, sin):
    stacked = jnp.concatenate([(cos * own).astype(BF16), (sin * partner).astype(BF16)], axis=0)
    return jnp.dot(matrix, stacked, preferred_element_type=F32)


def lane_partner(x, span):
    lo, hi = x[:, :LANES], x[:, LANES:]
    if span == LANES:
        return jnp.concatenate([hi, lo], axis=1)
    index = lax.broadcasted_iota(jnp.int32, lo.shape, 1)
    index = jnp.bitwise_xor(index, span)
    parts = [jnp.take_along_axis(p, index, axis=1, mode="promise_in_bounds") for p in (lo, hi)]
    return jnp.concatenate(parts, axis=1)


def kernel(
    n_box, src_hbm, proj_hbm, local_hbm, cross_hbm, ang_hbm, eval_hbm, out_ref,
    src_ref, proj_ref, local_ref, cross_ref, ang_ref, eval_t_ref, eval_ref,
    snd, rcv, aux, ang_out, local_w, in_sem, src_sem,
    s_snd, s_rcv, w_snd, w_rcv, a_snd, a_rcv, q_snd, q_rcv,
):
    bits = n_box.bit_length() - 1
    n_local, n_cross = local_ref.shape[0], cross_ref.shape[0]
    rank = proj_ref.shape[0]
    n_sub = rank // TILE
    group = src_hbm.shape[1] // n_box
    w_rows = n_cross * TILE
    me = lax.axis_index("box")
    part = lax.axis_index("src")

    def peer(d):
        return xor(me, d, bits)

    def to_box(d):
        return (peer(d), part)

    part_y, part_c = xor(part, 2, 2), xor(part, 1, 2)
    barrier = pltpu.get_barrier_semaphore()
    for target in [to_box(d) for d in range(1, n_box)] + [(me, part_y), (me, part_c)]:
        pl.semaphore_signal(barrier, inc=1, device_id=target, device_id_type=MESH)

    def load(i, source, target):
        return pltpu.make_async_copy(source, target, in_sem.at[i])

    loads = [
        load(i, *pair)
        for i, pair in enumerate([
            (proj_hbm, proj_ref), (ang_hbm, ang_ref), (local_hbm, local_ref),
            (cross_hbm, cross_ref), (eval_hbm, eval_t_ref),
        ])
    ]

    def columns(sub, d):
        return pl.ds(pl.multiple_of(peer(d) * group + sub * UNIT, UNIT), UNIT)

    def load_source(sub, d):
        return pltpu.make_async_copy(
            src_hbm.at[:, columns(sub, d)], src_ref.at[sub, d], src_sem.at[sub, d]
        )

    far = n_box // 2
    order = list(range(far, n_box)) + list(range(far - 1, -1, -1))

    def start_unit(sub):
        for d in order:
            load_source(sub, d).start()

    for copy in loads[:3]:
        copy.start()
    start_unit(0)
    for copy in loads[3:]:
        copy.start()

    def start_rest(it, carry):
        start_unit(it)
        return carry

    lax.fori_loop(1, n_sub, start_rest, 0)
    for copy in loads[:3]:
        copy.wait()
    for l in range(n_local):
        local_w[l] = jnp.concatenate([local_ref[l, 0], local_ref[l, 1]], axis=1)

    def angle_tile(d):
        block = ang_ref[:, columns(part, d)].astype(F32)[n_local:n_local + n_cross]
        block = jnp.concatenate([block, jnp.zeros((8 - n_cross, UNIT), F32)], axis=0)
        return jnp.concatenate([block[:, :LANES], block[:, LANES:]], axis=0).astype(BF16)

    def prepare_aux():
        for copy in loads[3:]:
            copy.wait()
        for m in range(n_cross):
            rows = pl.ds(pl.multiple_of(part * TILE, TILE), TILE)
            aux[part, me, m * TILE:(m + 1) * TILE, :] = jnp.concatenate(
                [cross_ref[m, 0, rows, :], cross_ref[m, 1, rows, :]], axis=1
            )
        aux[part, me, w_rows:w_rows + TILE, :] = angle_tile(0)
        for d in range(1, n_box):
            ang_out[d] = angle_tile(d)

    def w_copy(d):
        low = d if d <= far else d - far
        piece = aux.at[part, peer(d - low), 0:w_rows]
        return pltpu.make_async_remote_copy(
            src_ref=piece, dst_ref=piece, send_sem=w_snd.at[d], recv_sem=w_rcv.at[d],
            device_id=to_box(low), device_id_type=MESH,
        )

    def a_copy(d):
        return pltpu.make_async_remote_copy(
            src_ref=ang_out.at[d], dst_ref=aux.at[part, me, w_rows:w_rows + TILE],
            send_sem=a_snd.at[d], recv_sem=a_rcv.at[d],
            device_id=to_box(d), device_id_type=MESH,
        )

    def q_copy(i):
        quarter = part if i < 2 else part_y
        return pltpu.make_async_remote_copy(
            src_ref=aux.at[quarter], dst_ref=aux.at[quarter],
            send_sem=q_snd.at[i], recv_sem=q_rcv.at[i],
            device_id=(me, part_y if i == 0 else part_c), device_id_type=MESH,
        )

    def s_copy(sub, d):
        return pltpu.make_async_remote_copy(
            src_ref=snd.at[sub, d], dst_ref=rcv.at[sub, me],
            send_sem=s_snd.at[sub, d], recv_sem=s_rcv.at[sub, d],
            device_id=to_box(d), device_id_type=MESH,
        )

    def local_levels(chosen, midway, at=n_local // 2):
        xs, cs, ss = {}, {}, {}
        for sub, d in chosen:
            load_source(sub, d).wait()
        for sub, d in chosen:
            xs[d] = jnp.dot(proj_ref[...], src_ref[sub, d], preferred_element_type=F32)
            cs[d], ss[d] = cos_sin(ang_ref[:, columns(sub, d)].astype(F32)[:n_local])
        for l in range(n_local):
            if l == at:
                midway()
            matrix = local_w[l]
            for _, d in chosen:
                x = xs[d]
                xs[d] = mix(matrix, x, lane_partner(x, 1 << l), cs[d][l:l + 1], ss[d][l:l + 1])
        for sub, d in chosen:
            if d:
                snd[sub, d] = xs[d].astype(BF16)
                s_copy(sub, d).start()
            else:
                rcv[sub, me] = xs[0].astype(BF16)

    def send_aux():
        pl.semaphore_wait(barrier, n_box + 1)
        prepare_aux()
        for d in range(far, 0, -1):
            w_copy(d).start()
        for d in range(n_box - 1, 0, -1):
            a_copy(d).start()

    def forward_aux():
        w_copy(far).wait_recv()
        for d in range(far + 1, n_box):
            w_copy(d).start()

    def far_units(sub):
        return [(sub, d) for d in order[:far]]

    def near_units(sub):
        return [(sub, d) for d in order[far:]]

    local_levels(far_units(0), send_aux, n_local // 4)

    def local_step(sub, carry):
        def move_aux():
            @pl.when(sub == 1)
            def _():
                forward_aux()

            @pl.when(sub == 2)
            def _():
                for d in range(1, n_box):
                    if d != far:
                        w_copy(d).wait_recv()
                    a_copy(d).wait_recv()
                q_copy(0).start()
                q_copy(1).start()

        local_levels(far_units(sub) + near_units(sub - 1), move_aux)
        return carry

    def finish_aux():
        q_copy(0).wait_recv()
        q_copy(2).start()

    lax.fori_loop(1, n_sub, local_step, 0)
    local_levels(near_units(n_sub - 1), finish_aux)
    eval_ref[...] = eval_t_ref[...].astype(F32).T.astype(BF16)
    q_copy(1).wait_recv()
    q_copy(2).wait_recv()

    def cross_step(sub, carry):
        for d in range(1, n_box):
            s_copy(sub, d).wait_recv()
        xs = [rcv[sub, k].astype(F32) for k in range(n_box)]
        tables = [cos_sin(aux[sub, k, w_rows:w_rows + TILE, :].astype(F32)) for k in range(n_box)]

        def row(table, m):
            return jnp.concatenate([table[m:m + 1], table[8 + m:9 + m]], axis=1)

        for m in range(n_cross):
            bit = 1 << (bits - 1 - m) % bits
            new = []
            for k in range(n_box):
                matrix = jnp.concatenate(
                    [aux[q, k, m * TILE:(m + 1) * TILE, :] for q in range(n_sub)], axis=0
                )
                cos, sin = tables[k]
                new.append(mix(matrix, xs[k], xs[k ^ bit], row(cos, m), row(sin, m)))
            xs = new
        for k in range(n_box):
            pixels = jnp.dot(eval_ref[...], xs[k].astype(BF16), preferred_element_type=F32)
            start = pl.multiple_of(k * group + sub * UNIT, UNIT)
            out_ref[:, pl.ds(start, UNIT)] = pixels.astype(BF16)
        return carry

    lax.fori_loop(0, n_sub, cross_step, 0)

    def drain(sub, carry):
        for d in range(1, n_box):
            s_copy(sub, d).wait_send()
        return carry

    lax.fori_loop(0, n_sub, drain, 0)
    for d in range(1, n_box):
        w_copy(d).wait_send()
        a_copy(d).wait_send()
    for i in range(3):
        q_copy(i).wait_send()


def shards(source_field, project_mats, local_mats, cross_mats, angles, evaluate_mats):
    n_box = lax.axis_size("box")
    rank = project_mats.shape[0]
    n_sub = rank // TILE
    n_cross = cross_mats.shape[0]
    boxes = source_field.shape[1]
    pixels = evaluate_mats.shape[0]
    rows = n_cross * TILE + TILE
    dma = pltpu.SemaphoreType.DMA
    flops = 2 * boxes * rank * (2 * pixels + 2 * rank * angles.shape[0])
    return pl.pallas_call(
        functools.partial(kernel, n_box),
        out_shape=pltpu.VMEM((pixels, boxes), BF16),
        in_specs=[pl.BlockSpec(memory_space=pltpu.HBM)] * 6,
        out_specs=pl.BlockSpec(memory_space=pltpu.VMEM),
        scratch_shapes=[
            pltpu.VMEM((n_sub, n_box, pixels, UNIT), BF16),
            pltpu.VMEM(project_mats.shape, BF16),
            pltpu.VMEM(local_mats.shape, BF16),
            pltpu.VMEM(cross_mats.shape, BF16),
            pltpu.VMEM(angles.shape, BF16),
            pltpu.VMEM((rank, pixels), BF16),
            pltpu.VMEM((pixels, rank), BF16),
            pltpu.VMEM((n_sub, n_box, rank, UNIT), BF16),
            pltpu.VMEM((n_sub, n_box, rank, UNIT), BF16),
            pltpu.VMEM((n_sub, n_box, rows, LANES), BF16),
            pltpu.VMEM((n_box, TILE, LANES), BF16),
            pltpu.VMEM((local_mats.shape[0], rank, 2 * rank), BF16),
            dma((5,)), dma((n_sub, n_box)),
            dma((n_sub, n_box)), dma((n_sub, n_box)),
            dma((n_box,)), dma((n_box,)),
            dma((n_box,)), dma((n_box,)),
            dma((3,)), dma((3,)),
        ],
        compiler_params=pltpu.CompilerParams(
            collective_id=0, has_side_effects=True, vmem_limit_bytes=60 * 1024 * 1024
        ),
        cost_estimate=pl.CostEstimate(
            flops=flops, bytes_accessed=4 * boxes * pixels, transcendentals=0
        ),
    )(source_field, project_mats, local_mats, cross_mats, angles, evaluate_mats.T)


def fits_kernel(mesh):
    return mesh.shape["box"] == 8 and mesh.shape["src"] == 4


def solution(mesh):
    in_specs = (
        P("src", "box"),
        P("box", None),
        P(None, None, "box", None),
        P(None, None, "box", None),
        P(None, "box"),
        P("box", None),
    )
    out_specs = P("src", "box")
    body = shards if fits_kernel(mesh) else plain_shards
    return jax.shard_map(body, mesh=mesh, in_specs=in_specs, out_specs=out_specs, check_vma=False)
```
